256 devices in a mesh: dp: 128 (over x_lo, z, y, core), rows: 2 (over x_hi).
Axes of the slice: x: 4 (x_hi: 2, x_lo: 2; x = x_hi * 2 + x_lo), y: 4, z: 8, core: 2. Of those that a mesh axis runs over, the one named last changes fastest.
Arguments:
- latents: bfloat16 [128, 4, 128, 320], P('dp', 'rows'), may hold values from -6 to 6
- mean_one: float32 [128, 32], P('dp'), may hold values from -0.5 to 0.5
- rstd_one: float32 [128, 32], P('dp'), may hold values from 0.5 to 2
- gain_one: float32 [320], replicated, may hold values from 0.25 to 1.75
- shift_one: float32 [320], replicated, may hold values from -0.5 to 0.5
- kernel_one: bfloat16 [4, 9, 25600], P(None, None, 'dp'), may hold values from -0.109375 to 0.109375
- bias_one: float32 [320], replicated, may hold values from -3 to 3
- embed_bias: float32 [128, 320], P('dp'), may hold values from -3 to 3
- mean_two: float32 [128, 32], P('dp'), may hold values from -0.5 to 0.5
- rstd_two: float32 [128, 32], P('dp'), may hold values from 0.5 to 2
- gain_two: float32 [320], replicated, may hold values from 0.25 to 1.75
- shift_two: float32 [320], replicated, may hold values from -0.5 to 0.5
- kernel_two: bfloat16 [4, 9, 25600], P(None, None, 'dp'), may hold values from -0.109375 to 0.109375
- bias_two: float32 [320], replicated, may hold values from -3 to 3
Outputs:
- block_out: bfloat16 [128, 4, 128, 320], P('dp', 'rows')
The draws below stay inside these ranges and needn't reach their ends.
All inputs are finite; a program needn't handle non-finite values.
Results may differ from the reference program's by a relative error of at most 0.0045.
Values may be sent and summed in bfloat16 or wider, within the bound.
A program may use at most 192 MiB of HBM per device.

```python
import math
import jax
import jax.numpy as jnp
from jax import lax

C = 320
GROUPS = 32
SPANS = 4
COLS = 128
SPAN = 80
HEIGHT = 4
LATENTS = 128


def level_of(rng, extent, shards, least, high):
    loudness, own = 1.0, jax.random.fold_in(rng, 6)
    for dim, parts in shards:
        heights = jnp.exp(jax.random.uniform(jax.random.fold_in(own, dim), (parts,), jnp.float32, least / len(shards), high / len(shards)))
        loudness = loudness * jnp.repeat(heights, extent[dim] // parts).reshape([-1 if axis == dim else 1 for axis in range(len(extent))])
    return loudness


def bell_draw(own_key, dims, scale, bound, pieces=(), kind=jnp.bfloat16):
    values = scale * jax.random.normal(own_key, dims, jnp.float32)
    if pieces:
        values = values * level_of(own_key, dims, pieces, -0.22, 0.18)
    return jnp.clip(values, -bound, bound).astype(kind)


def setup_inputs(seed: int = 0) -> dict:
    key_of = jax.random.split(jax.random.key(seed), 15)
    return {
        "latents": bell_draw(key_of[0], (LATENTS, HEIGHT, COLS, C), 1.0, 6.0, ((0, 128), (1, 2))),
        "mean_one": jnp.clip(jax.random.uniform(key_of[1], (LATENTS, GROUPS), jnp.float32, -0.5, 0.5) * level_of(key_of[1], (LATENTS, GROUPS), ((0, 128),), -0.4, 0.0), -0.5, 0.5),
        "rstd_one": jnp.clip(jnp.exp(math.log(2.0) - 1.3862944 * jax.random.uniform(key_of[2], (LATENTS, GROUPS), jnp.float32) ** level_of(key_of[2], (LATENTS, GROUPS), ((0, 128),), -0.2, 0.2)), 0.5, 2.0),
        "gain_one": jnp.clip(1.0 + 0.15 * jax.random.normal(key_of[3], (C,), jnp.float32), 0.25, 1.75),
        "shift_one": jnp.clip(jax.random.uniform(key_of[4], (C,), jnp.float32, -0.5, 0.5), -0.5, 0.5),
        "kernel_one": bell_draw(key_of[5], (SPANS, 9, SPAN * C), (9 * C) ** -0.5, 0.109375, ((2, 128),)),
        "bias_one": bell_draw(key_of[6], (C,), 0.5, 3.0, (), jnp.float32),
        "embed_bias": bell_draw(key_of[7], (LATENTS, C), 0.5, 3.0, ((0, 128),), jnp.float32),
        "mean_two": jnp.clip(jax.random.uniform(key_of[8], (LATENTS, GROUPS), jnp.float32, -0.5, 0.5) * level_of(key_of[8], (LATENTS, GROUPS), ((0, 128),), -0.4, 0.0), -0.5, 0.5),
        "rstd_two": jnp.clip(jnp.exp(math.log(2.0) - 1.3862944 * jax.random.uniform(key_of[9], (LATENTS, GROUPS), jnp.float32) ** level_of(key_of[9], (LATENTS, GROUPS), ((0, 128),), -0.2, 0.2)), 0.5, 2.0),
        "gain_two": jnp.clip(1.0 + 0.15 * jax.random.normal(key_of[10], (C,), jnp.float32), 0.25, 1.75),
        "shift_two": jnp.clip(jax.random.uniform(key_of[11], (C,), jnp.float32, -0.5, 0.5), -0.5, 0.5),
        "kernel_two": bell_draw(key_of[12], (SPANS, 9, SPAN * C), (9 * C) ** -0.5, 0.109375, ((2, 128),)),
        "bias_two": bell_draw(key_of[13], (C,), 0.5, 3.0, (), jnp.float32),
    }


def norm_silu(values, group_mean, group_rstd, gain_vec, shift_vec):
    height, columns, channels = values.shape
    groups = group_mean.shape[0]
    grouped = values.reshape(height, columns, groups, channels // groups)
    scaled = (grouped - group_mean[:, None]) * group_rstd[:, None]
    return jax.nn.silu(scaled.reshape(height, columns, channels) * gain_vec + shift_vec)


def convolve(activation, kernel):
    channels = activation.shape[-1]
    blocks = kernel.shape[0]
    weights = kernel.astype(jnp.float32).reshape(blocks, 3, 3, channels // blocks, channels)
    weights = jnp.transpose(weights, (1, 2, 0, 3, 4)).reshape(3, 3, channels, channels)
    result = lax.conv_general_dilated(
        activation.astype(jnp.float32)[None], weights, (1, 1), ((1, 1), (1, 1)),
        dimension_numbers=("NHWC", "HWIO", "NHWC"), precision=lax.Precision.HIGHEST)
    return result[0]


def reference(latents, mean_one, rstd_one, gain_one, shift_one, kernel_one, bias_one, embed_bias,
              mean_two, rstd_two, gain_two, shift_two, kernel_two, bias_two):
    def one_latent(inputs):
        sample, first_mean, first_rstd, embedding, second_mean, second_rstd = inputs
        sample_f = sample.astype(jnp.float32)
        first_act = norm_silu(sample_f, first_mean, first_rstd, gain_one, shift_one).astype(jnp.bfloat16)
        hidden = convolve(first_act, kernel_one) + bias_one + embedding
        second_act = norm_silu(hidden, second_mean, second_rstd, gain_two, shift_two).astype(jnp.bfloat16)
        result = convolve(second_act, kernel_two) + bias_two + sample_f
        return result.astype(jnp.bfloat16)

    return lax.map(one_latent, (latents, mean_one, rstd_one, embed_bias, mean_two, rstd_two))
```

```python
from functools import partial

import jax
import jax.numpy as jnp
from jax import lax
from jax.experimental import pallas as pl
from jax.experimental.pallas import tpu as pltpu
from jax.sharding import PartitionSpec as P

MESH = pl.DeviceIdType.MESH
BF = jnp.bfloat16
F32 = jnp.float32
Z_STEPS = (1, -1, 2, -2, 3, -3, 4)
Y_STEPS = (1, -1, 2)
SWAPS = tuple((a, b) for a in range(4) for b in range(2) if (a, b) != (0, 0))
SLOT = 128


def device(x, y, z, c):
    x, y, z, c = x % 4, y % 4, z % 8, c % 2
    return ((((x % 2) * 8 + z) * 4 + y) * 2 + c, x // 2)


def silu_norm(values, mean, rstd, gain, shift):
    scaled = ((values - mean) * rstd) * gain + shift
    return scaled / (1.0 + jnp.exp(-scaled))


def spread(channel_values):
    group = lax.broadcasted_iota(jnp.int32, (32, 320), 0)
    lane = lax.broadcasted_iota(jnp.int32, (32, 320), 1)
    pick = jnp.where(lane // 10 == group, 1.0, 0.0).astype(F32)
    wide = jnp.broadcast_to(channel_values, (8, 32))
    return jnp.dot(wide, pick, precision=lax.Precision.HIGHEST, preferred_element_type=F32)[0:1]


def expand(act, pick, tap_lane):
    wide = jnp.dot(act, pick, preferred_element_type=F32)
    row = lax.broadcasted_iota(jnp.int32, (128, 1024), 0)
    before = jnp.where(row == 0, 0.0, pltpu.roll(wide, 1, 0))
    after = jnp.where(row == 127, 0.0, pltpu.roll(wide, 127, 0))
    return jnp.where(tap_lane < 5, before, jnp.where(tap_lane < 10, wide, after)).astype(BF)


def kernel(
    lat_ref, mean1, rstd1, gain1, shift1, k1_ref, bias1, embed, mean2, rstd2, gain2, shift2, k2_ref, bias2,
    out_ref,
    lat, msg, got, held, lhs, sample, pick, acc,
    lat_send, lat_recv, swap_send, swap_recv, z_send, z_recv, y_send, y_recv, x_send, x_recv, c_send, c_recv, local_sem,
):
    d = lax.axis_index("dp")
    h = lax.axis_index("rows")
    c = d % 2
    y = (d // 2) % 4
    z = (d // 8) % 8
    xl = d // 64
    x = 2 * h + xl

    barrier = pltpu.get_barrier_semaphore()
    partners = [device(x, y - a, z, c - b) for a, b in SWAPS]
    partners += [device(x, y, z - s, c) for s in Z_STEPS]
    partners += [device(x + s, y, z, c) for s in (1, 2, 3)]
    for partner in partners:
        pl.semaphore_signal(barrier, inc=1, device_id=partner, device_id_type=MESH)

    own_lat = pltpu.make_async_copy(lat_ref, lat.at[h], local_sem)
    own_lat.start()

    msg[...] = jnp.zeros_like(msg)
    for number, ref in enumerate((k1_ref, k2_ref)):
        raw = ref[...].astype(F32)
        for b in range(4):
            msg[b, number, 0:9, 0:200] = raw[:, b, :].astype(BF)

    lane = lax.broadcasted_iota(jnp.int32, (320, 1024), 1)
    channel = lax.broadcasted_iota(jnp.int32, (320, 1024), 0)
    group = lane // 16
    within = lane % 16
    wanted = (group % 4) * 80 + (group // 4) * 5 + within % 5
    pick[...] = jnp.where((wanted == channel) & (within < 15), 1.0, 0.0).astype(BF)

    pl.semaphore_wait(barrier, len(partners))

    swaps = []
    q = 2 * y + c
    for i, (a, b) in enumerate(SWAPS):
        to_y = (y + a) % 4
        copy = pltpu.make_async_remote_copy(
            src_ref=msg.at[to_y], dst_ref=got.at[q], send_sem=swap_send.at[i], recv_sem=swap_recv.at[i],
            device_id=device(x, y + a, z, c + b), device_id_type=MESH)
        copy.start()
        swaps.append(copy)
    lat_copy = pltpu.make_async_remote_copy(
        src_ref=lat_ref, dst_ref=lat.at[h], send_sem=lat_send, recv_sem=lat_recv,
        device_id=device(x + 2, y, z, c), device_id_type=MESH)
    lat_copy.start()
    got[q] = msg[y]

    for copy in swaps:
        copy.wait()

    col = lax.broadcasted_iota(jnp.int32, (16, 384), 1)
    row48 = lax.broadcasted_iota(jnp.int32, (48, 80), 0)
    col80 = lax.broadcasted_iota(jnp.int32, (48, 80), 1)
    in_tile = row48 % 16
    source = (in_tile % 5) * 16 + (row48 // 16) * 3 + in_tile // 5
    place = jnp.where((source == col80) & (in_tile < 15), 1.0, 0.0).astype(BF)
    whole = []
    for number in range(2):
        pieces = [
            jnp.concatenate([got[i, number].astype(F32), jnp.zeros((16, 128), F32)], axis=1) for i in range(8)
        ]
        rows = []
        for p in range(5):
            total = jnp.zeros((16, 384), F32)
            for i in range(8):
                by = 200 * i - 320 * p
                low, high = max(0, -by), min(200, 320 - by)
                if low < high:
                    part = jnp.where((col >= low) & (col < high), pieces[i], 0.0)
                    total = total + (pltpu.roll(part, by % 384, 1) if by % 384 else part)
            rows.append(total)
        stacked = jnp.concatenate(rows, axis=0).astype(BF)
        whole.append(jnp.dot(place, stacked, preferred_element_type=F32))
    one, two = whole
    slot = (xl * 8 + z) * 4 + y
    first = c == 0
    held[c, slot, 0:48] = jnp.where(first, one[:, 0:128], one[:, 128:256]).astype(BF)
    held[c, slot, 80:128] = jnp.where(first, two[:, 0:128], two[:, 128:256]).astype(BF)
    last = one[:, 256:384] + pltpu.roll(two[:, 256:384], 64, 1)
    held[c, slot, 48:80] = jnp.where(first, last[0:32], last[16:48]).astype(BF)

    copies = []
    for i, s in enumerate(Z_STEPS):
        copy = pltpu.make_async_remote_copy(
            src_ref=held.at[c, slot], dst_ref=held.at[c, slot], send_sem=z_send.at[i], recv_sem=z_recv.at[i],
            device_id=device(x, y, z + s, c), device_id_type=MESH)
        copy.start()
        copies.append(copy)

    own_lat.wait()
    lat_copy.wait()
    m1, r1 = spread(mean1[...]), spread(rstd1[...])
    tap_lane = lax.broadcasted_iota(jnp.int32, (128, 1024), 1) % 16
    g1, s1 = gain1[...].reshape(1, 320), shift1[...].reshape(1, 320)
    lhs[0] = jnp.zeros((128, 1024), BF)
    lhs[5] = jnp.zeros((128, 1024), BF)
    for r in range(4):
        values = lat[r // 2, r % 2].astype(F32).T
        sample[r] = values
        lhs[r + 1] = expand(silu_norm(values, m1, r1, g1, s1).astype(BF), pick[...], tap_lane)

    for copy in copies:
        copy.wait()
    copies = []
    for i, s in enumerate(Y_STEPS):
        for zz in range(8):
            place_of = (xl * 8 + zz) * 4 + y
            copy = pltpu.make_async_remote_copy(
                src_ref=held.at[c, place_of], dst_ref=held.at[c, place_of],
                send_sem=y_send.at[i, zz], recv_sem=y_recv.at[i, zz],
                device_id=device(x, y + s, z, c), device_id_type=MESH)
            copy.start()
            copies.append(copy)
    for copy in copies:
        copy.wait()
    copies = []
    half = pl.ds(xl * 32 + h * 16, 16)
    for i, s in enumerate((1, -1)):
        copy = pltpu.make_async_remote_copy(
            src_ref=held.at[c, half], dst_ref=held.at[c, half], send_sem=x_send.at[i], recv_sem=x_recv.at[i],
            device_id=device(x + s, y, z, c), device_id_type=MESH)
        copy.start()
        copies.append(copy)
    for copy in copies:
        copy.wait()
    copy = pltpu.make_async_remote_copy(
        src_ref=held.at[c], dst_ref=held.at[c], send_sem=c_send, recv_sem=c_recv,
        device_id=device(x, y, z, c + 1), device_id_type=MESH)
    copy.start()
    copy.wait()

    def weights(dy, base):
        t0 = held[0, :, base + 16 * dy : base + 16 * dy + 16].reshape(1024, 128)
        t1 = held[1, :, base + 16 * dy : base + 16 * dy + 16].reshape(1024, 128)
        owner, at = ((0, 48), (0, 64), (1, 64))[dy]
        t2 = held[owner, :, at : at + 16].reshape(1024, 128)
        return jnp.concatenate([t0, t1, t2], axis=1)

    for dy in range(3):
        left = lhs[pl.ds(h + dy, 3)].reshape(384, 1024)
        product = jnp.dot(left, weights(dy, 0), preferred_element_type=F32)
        if dy:
            acc[...] += product
        else:
            acc[...] = product

    m2, r2 = spread(mean2[...]), spread(rstd2[...])
    g2, s2 = gain2[...].reshape(1, 320), shift2[...].reshape(1, 320)
    offset = bias1[...].reshape(1, 320) + embed[...]
    for r in range(3):
        hidden = acc[128 * r : 128 * r + 128, 0:320] + offset
        lhs[r + 1] = expand(silu_norm(hidden, m2, r2, g2, s2).astype(BF), pick[...], tap_lane)
    lhs[4] = jnp.zeros((128, 1024), BF)
    for dy in range(3):
        left = lhs[pl.ds(h + dy, 2)].reshape(256, 1024)
        product = jnp.dot(left, weights(dy, 80), preferred_element_type=F32)
        if dy:
            acc[0:256] += product
        else:
            acc[0:256] = product
    b2 = bias2[...].reshape(1, 320)
    for r in range(2):
        rows = acc[128 * r : 128 * r + 128]
        result = jnp.concatenate([rows[:, 0:256], rows[:, 320:384]], axis=1)
        out_ref[r] = ((result + b2 + sample[2 * h + r]).T).astype(BF)


def shards(latents, mean_one, rstd_one, gain_one, shift_one, kernel_one, bias_one, embed_bias,
           mean_two, rstd_two, gain_two, shift_two, kernel_two, bias_two):
    lat = jnp.transpose(latents[0], (0, 2, 1))
    k1 = jnp.transpose(kernel_one, (1, 0, 2))
    k2 = jnp.transpose(kernel_two, (1, 0, 2))
    vmem = pl.BlockSpec(memory_space=pltpu.VMEM)
    out = pl.pallas_call(
        kernel,
        out_shape=jax.ShapeDtypeStruct((2, 320, 128), BF),
        in_specs=[pl.BlockSpec(memory_space=pl.ANY)] + [vmem] * 13,
        out_specs=vmem,
        scratch_shapes=[
            pltpu.VMEM((2, 2, 320, 128), BF),
            pltpu.VMEM((4, 2, 16, 256), BF),
            pltpu.VMEM((8, 2, 16, 256), BF),
            pltpu.VMEM((2, 64, SLOT, 128), BF),
            pltpu.VMEM((6, 128, 1024), BF),
            pltpu.VMEM((4, 128, 320), F32),
            pltpu.VMEM((320, 1024), BF),
            pltpu.VMEM((384, 384), F32),
            pltpu.SemaphoreType.DMA, pltpu.SemaphoreType.DMA,
            pltpu.SemaphoreType.DMA((7,)), pltpu.SemaphoreType.DMA((7,)),
            pltpu.SemaphoreType.DMA((7,)), pltpu.SemaphoreType.DMA((7,)),
            pltpu.SemaphoreType.DMA((3, 8)), pltpu.SemaphoreType.DMA((3, 8)),
            pltpu.SemaphoreType.DMA((2,)), pltpu.SemaphoreType.DMA((2,)),
            pltpu.SemaphoreType.DMA, pltpu.SemaphoreType.DMA,
            pltpu.SemaphoreType.DMA,
        ],
        compiler_params=pltpu.CompilerParams(
            collective_id=0, has_side_effects=True, vmem_limit_bytes=40 * 2**20),
        name="residual_block",
    )(lat, mean_one, rstd_one, gain_one, shift_one, k1, bias_one, embed_bias,
      mean_two, rstd_two, gain_two, shift_two, k2, bias_two)
    return jnp.transpose(out, (0, 2, 1))[None]


def solution(mesh):
    placed = (
        P("dp", "rows", None, None), P("dp", None), P("dp", None), P(), P(), P(None, None, "dp"), P(),
        P("dp", None), P("dp", None), P("dp", None), P(), P(), P(None, None, "dp"), P(),
    )
    return jax.shard_map(
        shards, mesh=mesh, in_specs=placed, out_specs=P("dp", "rows", None, None), check_vma=False
    )
```

```python
from functools import partial

import jax
import jax.numpy as jnp
from jax import lax
from jax.experimental import pallas as pl
from jax.experimental.pallas import tpu as pltpu
from jax.sharding import PartitionSpec as P

MESH = pl.DeviceIdType.MESH
BF = jnp.bfloat16
F32 = jnp.float32
REL = (0, 1, -1, 2, -2, 3, -3, 4)
CHUNKS_A = ((0, 1), (1, 3), (3, 5), (5, 8))
CHUNKS_B = ((0, 5), (5, 8))
PART_A = (0, 96)
PART_B = (96, 128)
COPIES = 160
SWAPS = tuple((a, b) for a in range(4) for b in range(2) if (a, b) != (0, 0))
SLOT = 128


def device(x, y, z, c):
    x, y, z, c = x % 4, y % 4, z % 8, c % 2
    return ((((x % 2) * 8 + z) * 4 + y) * 2 + c, x // 2)


def silu_norm(values, mean, rstd, gain, shift):
    scaled = ((values - mean) * rstd) * gain + shift
    return scaled / (1.0 + jnp.exp(-scaled))


def spread(channel_values):
    group = lax.broadcasted_iota(jnp.int32, (32, 320), 0)
    lane = lax.broadcasted_iota(jnp.int32, (32, 320), 1)
    pick = jnp.where(lane // 10 == group, 1.0, 0.0).astype(F32)
    wide = jnp.broadcast_to(channel_values, (8, 32))
    return jnp.dot(wide, pick, precision=lax.Precision.HIGHEST, preferred_element_type=F32)[0:1]


def expand(act, pick, tap_lane):
    wide = jnp.dot(act, pick, preferred_element_type=F32)
    row = lax.broadcasted_iota(jnp.int32, (128, 1024), 0)
    before = jnp.where(row == 0, 0.0, pltpu.roll(wide, 1, 0))
    after = jnp.where(row == 127, 0.0, pltpu.roll(wide, 127, 0))
    return jnp.where(tap_lane < 5, before, jnp.where(tap_lane < 10, wide, after)).astype(BF)


def distance(place):
    return ((place + 1) // 2) * (2 * (place % 2) - 1)


def kernel(
    lat_ref, mean1, rstd1, gain1, shift1, k1_ref, bias1, embed, mean2, rstd2, gain2, shift2, k2_ref, bias2,
    out_ref,
    lat, raw, vectors, stats, msg, got, held, lhs, sample, pick, acc,
    lat_send, lat_recv, swap_send, swap_recv, sent, landed, local_sem,
):
    d = lax.axis_index("dp")
    h = lax.axis_index("rows")
    c = d % 2
    y = (d // 2) % 4
    z = (d // 8) % 8
    xl = d // 64
    x = 2 * h + xl

    local = []
    for i, (source, target) in enumerate((
        (k1_ref, raw.at[0]), (k2_ref, raw.at[1]), (lat_ref, lat.at[h]),
        (mean1, stats.at[0]), (rstd1, stats.at[1]), (mean2, stats.at[2]), (rstd2, stats.at[3]),
        (gain1, vectors.at[0]), (shift1, vectors.at[1]), (bias1, vectors.at[2]),
        (gain2, vectors.at[3]), (shift2, vectors.at[4]), (bias2, vectors.at[5]), (embed, vectors.at[pl.ds(6, 1)]),
    )):
        copy = pltpu.make_async_copy(source, target, local_sem.at[i])
        copy.start()
        local.append(copy)

    barrier = pltpu.get_barrier_semaphore()
    partners = [device(x, y - a, z, c - b) for a, b in SWAPS]
    partners += [device(x, y, z - s, c) for s in REL[1:]]
    partners += [device(x + s, y, z, c) for s in (1, 2, 3)]
    for partner in partners:
        pl.semaphore_signal(barrier, inc=1, device_id=partner, device_id_type=MESH)

    with jax.named_scope("messages"):
        msg[...] = jnp.zeros_like(msg)
        for number in range(2):
            local[number].wait()
            block = raw[number].astype(F32)
            for b in range(4):
                msg[b, number, 0:9, 0:200] = block[:, b, :].astype(BF)

    with jax.named_scope("barrier"):
        pl.semaphore_wait(barrier, len(partners))

    swaps = []
    q = 2 * y + c
    for i, (a, b) in enumerate(SWAPS):
        to_y = (y + a) % 4
        copy = pltpu.make_async_remote_copy(
            src_ref=msg.at[to_y], dst_ref=got.at[q], send_sem=swap_send.at[i], recv_sem=swap_recv.at[i],
            device_id=device(x, y + a, z, c + b), device_id_type=MESH)
        copy.start()
        swaps.append(copy)
    lat_copy = pltpu.make_async_remote_copy(
        src_ref=lat_ref, dst_ref=lat.at[h], send_sem=lat_send, recv_sem=lat_recv,
        device_id=device(x + 2, y, z, c), device_id_type=MESH)
    lat_copy.start()
    got[q] = msg[y]

    with jax.named_scope("pick"):
        lane = lax.broadcasted_iota(jnp.int32, (1, 1024), 1)
        within = lane % 16
        group = lane // 16
        zz = (z + distance(group % 8) + 8) % 8
        bb = (y + distance((group // 8) % 4) + 4) % 4
        xx = (xl + group // 32) % 2
        wanted = jnp.where(within < 15, bb * 80 + (xx * 8 + zz) * 5 + within % 5, -1)
        channel = lax.broadcasted_iota(jnp.int32, (320, 1024), 0)
        pick[...] = jnp.where(wanted == channel, 1.0, 0.0).astype(BF)

    with jax.named_scope("swap"):
        for copy in swaps:
            copy.wait_recv()

    with jax.named_scope("assemble"):
        col = lax.broadcasted_iota(jnp.int32, (16, 384), 1)
        row48 = lax.broadcasted_iota(jnp.int32, (48, 80), 0)
        col80 = lax.broadcasted_iota(jnp.int32, (48, 80), 1)
        in_tile = row48 % 16
        source = (in_tile % 5) * 16 + (row48 // 16) * 3 + in_tile // 5
        place = jnp.where((source == col80) & (in_tile < 15), 1.0, 0.0).astype(BF)
        whole = []
        for number in range(2):
            pieces = [
                jnp.concatenate([got[i, number].astype(F32), jnp.zeros((16, 128), F32)], axis=1) for i in range(8)
            ]
            rows = []
            for p in range(5):
                total = jnp.zeros((16, 384), F32)
                for i in range(8):
                    by = 200 * i - 320 * p
                    low, high = max(0, -by), min(200, 320 - by)
                    if low < high:
                        part = jnp.where((col >= low) & (col < high), pieces[i], 0.0)
                        total = total + (pltpu.roll(part, by % 384, 1) if by % 384 else part)
                rows.append(total)
            stacked = jnp.concatenate(rows, axis=0).astype(BF)
            whole.append(jnp.dot(place, stacked, preferred_element_type=F32))
        one, two = whole
        first = c == 0
        own = held.at[0, 0, 0, 0]
        own[0:48] = jnp.where(first, one[:, 0:128], one[:, 128:256]).astype(BF)
        own[80:128] = jnp.where(first, two[:, 0:128], two[:, 128:256]).astype(BF)
        last = one[:, 256:384] + pltpu.roll(two[:, 256:384], 64, 1)
        own[48:80] = jnp.where(first, last[0:32], last[16:48]).astype(BF)

    copies = []
    count = [0]

    def send(source, target, to, recv=None):
        i = len(copies)
        if recv is None:
            recv = landed.at[count[0]]
            count[0] += 1
        copy = pltpu.make_async_remote_copy(
            src_ref=source, dst_ref=target, send_sem=sent.at[i], recv_sem=recv, device_id=to, device_id_type=MESH)
        copy.start()
        copies.append(copy)
        return copy

    class Part:
        def __init__(self, span, chunks):
            self.low, self.high = span
            self.size = self.high - self.low
            self.half = pl.ds(self.low + h * (self.size // 2), self.size // 2)
            self.chunks = chunks
            self.z, self.y, self.yy, self.x, self.c = {}, {}, {}, {}, []

        def at(self, xr, yr, chunk, core=0):
            ys = yr if isinstance(yr, int) else pl.ds(yr[0], yr[1] - yr[0])
            low, high = chunk
            return held.at[core, xr, ys, pl.ds(low, high - low), pl.ds(self.low, self.size)]

        def half_at(self, xr, yr, chunk):
            low, high = chunk
            return held.at[0, xr, pl.ds(yr[0], yr[1] - yr[0]), pl.ds(low, high - low), self.half]

        def send_z(self):
            for i in range(1, 8):
                back = REL.index(-REL[i]) if REL[i] != 4 else 7
                self.z[back] = send(self.at(0, 0, (0, 1)), self.at(0, 0, (back, back + 1)), device(x, y, z + REL[i], c))

        def send_y(self, k):
            chunk = self.chunks[k]
            up = send(self.at(0, 0, chunk), self.at(0, 2, chunk), device(x, y + 1, z, c))
            down = send(self.at(0, 0, chunk), self.at(0, 1, chunk), device(x, y - 1, z, c))
            self.y[k] = (up, down)

        def send_x(self, k, ys):
            chunk = self.chunks[k]
            base = count[0]
            count[0] += 2
            for s in (1, -1):
                copy = send(self.half_at(0, ys, chunk), self.half_at(1, ys, chunk), device(x + s, y, z, c),
                            landed.at[base + h])
            self.x.setdefault(k, []).append((base, copy, ys))

        def wait_x(self, k):
            for base, copy, ys in self.x[k]:
                for side in range(2):
                    ref = self.half_at(1, ys, self.chunks[k])
                    pltpu.make_async_remote_copy(
                        src_ref=ref, dst_ref=ref, send_sem=sent.at[0], recv_sem=landed.at[base + side],
                        device_id=device(x + 1, y, z, c), device_id_type=MESH).wait_recv()

        def send_c(self, k, xr):
            chunk = self.chunks[k]
            self.c.append(send(self.at(xr, (0, 4), chunk), self.at(xr, (0, 4), chunk, 1), device(x, y, z, c + 1)))

        def after_z(self, k):
            for i in range(*self.chunks[k]):
                if i:
                    self.z[i].wait_recv()
            self.send_y(k)
            self.send_x(k, (0, 1))

        def after_y(self, k):
            for copy in self.y[k]:
                copy.wait_recv()
            chunk = self.chunks[k]
            if k in (0, 3) or (len(self.chunks) == 2 and k == 1):
                self.yy[k] = send(self.at(0, 2, chunk), self.at(0, 3, chunk), device(x, y + 1, z, c))
            else:
                self.yy[k] = send(self.at(0, 1, chunk), self.at(0, 3, chunk), device(x, y - 1, z, c))
            self.send_x(k, (1, 3))

        def after_yy(self, k):
            self.yy[k].wait_recv()
            self.send_x(k, (3, 4))
            self.send_c(k, 0)

        def after_x(self, k):
            self.wait_x(k)
            self.send_c(k, 1)

    a, b = Part(PART_A, CHUNKS_A), Part(PART_B, CHUNKS_B)
    with jax.named_scope("send_first"):
        a.send_z()
        a.after_z(0)
        b.send_z()

    tap_lane = lax.broadcasted_iota(jnp.int32, (128, 1024), 1) % 16

    def vector(i):
        return vectors[i : i + 1]

    with jax.named_scope("gather_1"):
        a.after_z(1)
        a.after_y(0)
        a.after_z(2)
    with jax.named_scope("stats"):
        for copy in local[2:]:
            copy.wait()
        lat_copy.wait_recv()
        m1, r1 = spread(stats[0]), spread(stats[1])
        m2, r2 = spread(stats[2]), spread(stats[3])
        lhs[0] = jnp.zeros((128, 1024), BF)
        lhs[5] = jnp.zeros((128, 1024), BF)

    def activate(r):
        with jax.named_scope("activate"):
            values = lat[r // 2, r % 2].astype(F32).T
            sample[r] = values
            lhs[r + 1] = expand(silu_norm(values, m1, r1, vector(0), vector(1)).astype(BF), pick[...], tap_lane)

    with jax.named_scope("gather_2"):
        a.after_y(1)
        a.after_z(3)
    activate(0)
    with jax.named_scope("gather_3"):
        a.after_yy(0)
        a.after_y(2)
        b.after_z(0)
    activate(1)
    with jax.named_scope("gather_4"):
        a.after_yy(1)
        a.after_y(3)
        b.after_z(1)
    activate(2)
    with jax.named_scope("gather_5"):
        a.after_yy(2)
        b.after_y(0)
        a.after_x(0)
        a.after_yy(3)
        b.after_y(1)
    activate(3)
    with jax.named_scope("gather_6"):
        a.after_x(1)
        b.after_yy(0)
        a.after_x(2)
        b.after_yy(1)
        a.after_x(3)
    with jax.named_scope("sibling_a"):
        for copy in a.c:
            copy.wait_recv()

    def weights(dy, base):
        t0 = held[c, :, :, :, base + 16 * dy : base + 16 * dy + 16].reshape(1024, 128)
        t1 = held[1 - c, :, :, :, base + 16 * dy : base + 16 * dy + 16].reshape(1024, 128)
        owner, at = ((c, 48), (c, 64), (1 - c, 64))[dy]
        t2 = held[owner, :, :, :, at : at + 16].reshape(1024, 128)
        return jnp.concatenate([t0, t1, t2], axis=1)

    with jax.named_scope("conv_one"):
        for dy in range(3):
            left = lhs[pl.ds(h + dy, 3)].reshape(384, 1024)
            product = jnp.dot(left, weights(dy, 0), preferred_element_type=F32)
            if dy:
                acc[...] += product
            else:
                acc[...] = product

    with jax.named_scope("gather_b"):
        for k in range(len(CHUNKS_B)):
            b.after_x(k)

    with jax.named_scope("second_activation"):
        offset = vector(2) + vector(6)
        for r in range(3):
            hidden = acc[128 * r : 128 * r + 128, 0:320] + offset
            lhs[r + 1] = expand(silu_norm(hidden, m2, r2, vector(3), vector(4)).astype(BF), pick[...], tap_lane)
        lhs[4] = jnp.zeros((128, 1024), BF)
    with jax.named_scope("sibling_b"):
        for copy in b.c:
            copy.wait_recv()
    with jax.named_scope("conv_two"):
        for dy in range(3):
            left = lhs[pl.ds(h + dy, 2)].reshape(256, 1024)
            product = jnp.dot(left, weights(dy, 80), preferred_element_type=F32)
            if dy:
                acc[0:256] += product
            else:
                acc[0:256] = product
    with jax.named_scope("result"):
        for r in range(2):
            rows = acc[128 * r : 128 * r + 128]
            result = jnp.concatenate([rows[:, 0:256], rows[:, 320:384]], axis=1)
            out_ref[r] = ((result + vector(5) + sample[2 * h + r]).T).astype(BF)
    with jax.named_scope("sends"):
        for copy in swaps + [lat_copy] + copies:
            copy.wait_send()


def shards(latents, mean_one, rstd_one, gain_one, shift_one, kernel_one, bias_one, embed_bias,
           mean_two, rstd_two, gain_two, shift_two, kernel_two, bias_two):
    lat = jnp.transpose(latents[0], (0, 2, 1))
    k1 = jnp.transpose(kernel_one, (1, 0, 2))
    k2 = jnp.transpose(kernel_two, (1, 0, 2))
    vmem = pl.BlockSpec(memory_space=pltpu.VMEM)
    out = pl.pallas_call(
        kernel,
        out_shape=jax.ShapeDtypeStruct((2, 320, 128), BF),
        in_specs=[pl.BlockSpec(memory_space=pltpu.HBM)] * 14,
        out_specs=vmem,
        scratch_shapes=[
            pltpu.VMEM((2, 2, 320, 128), BF),
            pltpu.VMEM((2, 9, 4, 200), BF),
            pltpu.VMEM((8, 320), F32),
            pltpu.VMEM((4, 1, 32), F32),
            pltpu.VMEM((4, 2, 16, 256), BF),
            pltpu.VMEM((8, 2, 16, 256), BF),
            pltpu.VMEM((2, 2, 4, 8, SLOT, 128), BF),
            pltpu.VMEM((6, 128, 1024), BF),
            pltpu.VMEM((4, 128, 320), F32),
            pltpu.VMEM((320, 1024), BF),
            pltpu.VMEM((384, 384), F32),
            pltpu.SemaphoreType.DMA, pltpu.SemaphoreType.DMA,
            pltpu.SemaphoreType.DMA((7,)), pltpu.SemaphoreType.DMA((7,)),
            pltpu.SemaphoreType.DMA((COPIES,)), pltpu.SemaphoreType.DMA((COPIES,)),
            pltpu.SemaphoreType.DMA((14,)),
        ],
        compiler_params=pltpu.CompilerParams(
            collective_id=0, has_side_effects=True, vmem_limit_bytes=60 * 2**20),
        name="residual_block",
    )(lat, mean_one, rstd_one, gain_one, shift_one, k1, bias_one, embed_bias,
      mean_two, rstd_two, gain_two, shift_two, k2, bias_two)
    return jnp.transpose(out, (0, 2, 1))[None]


def solution(mesh):
    placed = (
        P("dp", "rows", None, None), P("dp", None), P("dp", None), P(), P(), P(None, None, "dp"), P(),
        P("dp", None), P("dp", None), P("dp", None), P(), P(), P(None, None, "dp"), P(),
    )
    return jax.shard_map(
        shards, mesh=mesh, in_specs=placed, out_specs=P("dp", "rows", None, None), check_vma=False
    )
```

```python
from functools import partial

import jax
import jax.numpy as jnp
from jax import lax
from jax.experimental import pallas as pl
from jax.experimental.pallas import tpu as pltpu
from jax.sharding import PartitionSpec as P

MESH = pl.DeviceIdType.MESH
BF = jnp.bfloat16
F32 = jnp.float32
REL = (0, 1, -1, 2, -2, 3, -3, 4)
CHUNKS = ((0, 1), (1, 3), (3, 5), (5, 7), (7, 8))
Z_ORDER = (1, 2, 3, 4, 5, 6, 7)
FAR = ()
COPIES = 64
SWAPS = tuple((a, b) for a in range(4) for b in range(2) if (a, b) != (0, 0))
SLOT = 128


def device(x, y, z, c):
    x, y, z, c = x % 4, y % 4, z % 8, c % 2
    return ((((x % 2) * 8 + z) * 4 + y) * 2 + c, x // 2)


def silu_norm(values, mean, rstd, gain, shift):
    scaled = ((values - mean) * rstd) * gain + shift
    return scaled / (1.0 + jnp.exp(-scaled))


def spread(channel_values):
    group = lax.broadcasted_iota(jnp.int32, (32, 320), 0)
    lane = lax.broadcasted_iota(jnp.int32, (32, 320), 1)
    pick = jnp.where(lane // 10 == group, 1.0, 0.0).astype(F32)
    wide = jnp.broadcast_to(channel_values, (8, 32))
    return jnp.dot(wide, pick, precision=lax.Precision.HIGHEST, preferred_element_type=F32)[0:1]


def expand(act, pick, tap_lane):
    wide = jnp.dot(act, pick, preferred_element_type=F32)
    row = lax.broadcasted_iota(jnp.int32, (128, 1024), 0)
    before = jnp.where(row == 0, 0.0, pltpu.roll(wide, 1, 0))
    after = jnp.where(row == 127, 0.0, pltpu.roll(wide, 127, 0))
    return jnp.where(tap_lane < 5, before, jnp.where(tap_lane < 10, wide, after)).astype(BF)


def distance(place):
    return ((place + 1) // 2) * (2 * (place % 2) - 1)


def kernel(
    lat_ref, mean1, rstd1, gain1, shift1, k1_ref, bias1, embed, mean2, rstd2, gain2, shift2, k2_ref, bias2,
    out_ref,
    lat, raw, vectors, stats, msg, got, held, lhs, sample, pick, acc,
    lat_send, lat_recv, swap_send, swap_recv, sent, landed, local_sem,
):
    d = lax.axis_index("dp")
    h = lax.axis_index("rows")
    c = d % 2
    y = (d // 2) % 4
    z = (d // 8) % 8
    xl = d // 64
    x = 2 * h + xl

    local = []
    for i, (source, target) in enumerate((
        (k1_ref, raw.at[0]), (k2_ref, raw.at[1]), (lat_ref, lat.at[h]),
        (mean1, stats.at[0]), (rstd1, stats.at[1]), (mean2, stats.at[2]), (rstd2, stats.at[3]),
        (gain1, vectors.at[0]), (shift1, vectors.at[1]), (bias1, vectors.at[2]),
        (gain2, vectors.at[3]), (shift2, vectors.at[4]), (bias2, vectors.at[5]), (embed, vectors.at[pl.ds(6, 1)]),
    )):
        copy = pltpu.make_async_copy(source, target, local_sem.at[i])
        copy.start()
        local.append(copy)

    barrier = pltpu.get_barrier_semaphore()
    partners = [device(x, y - a, z, c - b) for a, b in SWAPS]
    partners += [device(x, y, z - s, c) for s in REL[1:]]
    partners += [device(x + s, y, z, c) for s in (1, 2, 3)]
    for partner in partners:
        pl.semaphore_signal(barrier, inc=1, device_id=partner, device_id_type=MESH)

    msg[...] = jnp.zeros_like(msg)
    for number in range(2):
        local[number].wait()
        block = raw[number].astype(F32)
        for b in range(4):
            msg[b, number, 0:9, 0:200] = block[:, b, :].astype(BF)

    pl.semaphore_wait(barrier, len(partners))

    swaps = []
    q = 2 * y + c
    for i, (a, b) in enumerate(SWAPS):
        copy = pltpu.make_async_remote_copy(
            src_ref=msg.at[(y + a + 2 * h) % 4], dst_ref=got.at[q], send_sem=swap_send.at[i], recv_sem=swap_recv.at[i],
            device_id=device(x, y + a, z, c + b), device_id_type=MESH)
        copy.start()
        swaps.append(copy)
    lat_copy = pltpu.make_async_remote_copy(
        src_ref=lat_ref, dst_ref=lat.at[h], send_sem=lat_send, recv_sem=lat_recv,
        device_id=device(x + 2, y, z, c), device_id_type=MESH)
    lat_copy.start()
    got[q] = msg[(y + 2 * h) % 4]

    lane = lax.broadcasted_iota(jnp.int32, (1, 1024), 1)
    within = lane % 16
    group = lane // 16
    zz = (z + distance(group % 8) + 8) % 8
    side = group // 32
    row = (group // 8) % 4
    bb = (y + jnp.where(side == 0, distance(row) + 2 * h, row) + 4) % 4
    xx = (xl + side) % 2
    wanted = jnp.where(within < 15, bb * 80 + (xx * 8 + zz) * 5 + within % 5, -1)
    channel = lax.broadcasted_iota(jnp.int32, (320, 1024), 0)
    pick[...] = jnp.where(wanted == channel, 1.0, 0.0).astype(BF)

    tap_lane = lax.broadcasted_iota(jnp.int32, (128, 1024), 1) % 16

    def vector(i):
        return vectors[i : i + 1]

    for copy in local[2:]:
        copy.wait()
    m1, r1 = spread(stats[0]), spread(stats[1])
    m2, r2 = spread(stats[2]), spread(stats[3])
    lhs[0] = jnp.zeros((128, 1024), BF)
    lhs[5] = jnp.zeros((128, 1024), BF)

    def activate(half, r):
        values = lat[half, r].astype(F32).T
        sample[2 * half + r] = values
        lhs[2 * half + r + 1] = expand(
            silu_norm(values, m1, r1, vector(0), vector(1)).astype(BF), pick[...], tap_lane)

    activate(h, 0)
    activate(h, 1)

    for copy in swaps:
        copy.wait_recv()

    col = lax.broadcasted_iota(jnp.int32, (16, 384), 1)
    row48 = lax.broadcasted_iota(jnp.int32, (48, 80), 0)
    col80 = lax.broadcasted_iota(jnp.int32, (48, 80), 1)
    in_tile = row48 % 16
    source = (in_tile % 5) * 16 + (row48 // 16) * 3 + in_tile // 5
    place = jnp.where((source == col80) & (in_tile < 15), 1.0, 0.0).astype(BF)
    whole = []
    for number in range(2):
        pieces = [
            jnp.concatenate([got[i, number].astype(F32), jnp.zeros((16, 128), F32)], axis=1) for i in range(8)
        ]
        rows = []
        for p in range(5):
            total = jnp.zeros((16, 384), F32)
            for i in range(8):
                by = 200 * i - 320 * p
                low, high = max(0, -by), min(200, 320 - by)
                if low < high:
                    part = jnp.where((col >= low) & (col < high), pieces[i], 0.0)
                    total = total + (pltpu.roll(part, by % 384, 1) if by % 384 else part)
            rows.append(total)
        stacked = jnp.concatenate(rows, axis=0).astype(BF)
        whole.append(jnp.dot(place, stacked, preferred_element_type=F32))
    one, two = whole
    first = c == 0
    own = held.at[0, 0, 0, 0]
    own[0:48] = jnp.where(first, one[:, 0:128], one[:, 128:256]).astype(BF)
    own[80:128] = jnp.where(first, two[:, 0:128], two[:, 128:256]).astype(BF)
    last = one[:, 256:384] + pltpu.roll(two[:, 256:384], 64, 1)
    own[48:80] = jnp.where(first, last[0:32], last[16:48]).astype(BF)

    up, down, far = device(x, y + 1, z, c), device(x, y - 1, z, c), device(x, y + 2, z, c)
    right, left, sibling = device(x + 1, y, z, c), device(x - 1, y, z, c), device(x, y, z, c + 1)
    copies = []
    count = [0]

    def send(source, target, to, recv=None):
        i = len(copies)
        if recv is None:
            recv = landed.at[count[0]]
            count[0] += 1
        copy = pltpu.make_async_remote_copy(
            src_ref=source, dst_ref=target, send_sem=sent.at[i], recv_sem=recv, device_id=to, device_id_type=MESH)
        copy.start()
        copies.append(copy)
        return copy

    def at(xr, yr, chunk, core=0):
        low, high = chunk
        return held.at[core, xr, yr, pl.ds(low, high - low)]

    z_copies, y_copies, far_copies, x_copies, core_copies = {}, {}, {}, {}, ({}, {})

    def send_z():
        for i in Z_ORDER:
            back = REL.index(-REL[i]) if REL[i] != 4 else 7
            z_copies[back] = send(at(0, 0, (0, 1)), at(0, 0, (back, back + 1)), device(x, y, z + REL[i], c))

    def send_x(k, j):
        base = count[0]
        count[0] += 2
        for to in (right, left):
            send(at(0, j, CHUNKS[k]), at(1, 2 * h + j, CHUNKS[k]), to, landed.at[base + h])
        x_copies.setdefault(k, []).append(base)

    def send_core(k, xr):
        ys = pl.ds(0, 4)
        core_copies[xr][k] = send(at(xr, ys, CHUNKS[k]), at(xr, ys, CHUNKS[k], 1), sibling)

    def after_z(k):
        chunk = CHUNKS[k]
        for i in range(*chunk):
            if i:
                z_copies[i].wait_recv()
        y_copies[k] = send(at(0, 0, chunk), at(0, 1, chunk), down), send(at(0, 0, chunk), at(0, 2, chunk), up)
        if k in FAR:
            far_copies[k] = send(at(0, 0, chunk), at(0, 3, chunk), far)
        send_x(k, 0)

    def after_y(k):
        chunk = CHUNKS[k]
        from_up, from_down = y_copies[k]
        from_up.wait_recv()
        if k % 2 and k not in FAR:
            far_copies[k] = send(at(0, 1, chunk), at(0, 3, chunk), down)
        send_x(k, 1)
        from_down.wait_recv()
        if k % 2 == 0 and k not in FAR:
            far_copies[k] = send(at(0, 2, chunk), at(0, 3, chunk), up)

    def after_far(k):
        far_copies[k].wait_recv()
        send_core(k, 0)

    def after_x(k):
        for base in x_copies[k]:
            for side in range(2):
                ref = at(1, 0, CHUNKS[k])
                pltpu.make_async_remote_copy(
                    src_ref=ref, dst_ref=ref, send_sem=sent.at[0], recv_sem=landed.at[base + side],
                    device_id=right, device_id_type=MESH).wait_recv()
        send_core(k, 1)

    send_z()
    after_z(0)
    lat_copy.wait_recv()
    activate(1 - h, 0)
    after_z(1)
    after_y(0)
    activate(1 - h, 1)
    after_z(2)
    after_y(1)
    after_z(3)
    after_far(0)
    after_z(4)
    after_y(2)
    after_far(1)
    after_y(3)
    after_y(4)
    after_far(2)
    after_x(0)
    after_x(1)
    after_far(3)
    after_far(4)
    after_x(2)
    after_x(3)
    after_x(4)

    def weights(dy, base, half):
        t0 = held[c, half, :, :, base + 16 * dy : base + 16 * dy + 16].reshape(512, 128)
        t1 = held[1 - c, half, :, :, base + 16 * dy : base + 16 * dy + 16].reshape(512, 128)
        owner, row = ((c, 48), (c, 64), (1 - c, 64))[dy]
        t2 = held[owner, half, :, :, row : row + 16].reshape(512, 128)
        return jnp.concatenate([t0, t1, t2], axis=1)

    def convolve(rows, base, half):
        for dy in range(3):
            left_side = lhs[pl.ds(h + dy, rows), :, 512 * half : 512 * half + 512].reshape(128 * rows, 512)
            product = jnp.dot(left_side, weights(dy, base, half), preferred_element_type=F32)
            if dy or half:
                acc[0 : 128 * rows] += product
            else:
                acc[0 : 128 * rows] = product

    for copy in core_copies[0].values():
        copy.wait_recv()
    convolve(3, 0, 0)
    for copy in core_copies[1].values():
        copy.wait_recv()
    convolve(3, 0, 1)

    offset = vector(2) + vector(6)
    for r in range(3):
        hidden = acc[128 * r : 128 * r + 128, 0:320] + offset
        lhs[r + 1] = expand(silu_norm(hidden, m2, r2, vector(3), vector(4)).astype(BF), pick[...], tap_lane)
    lhs[4] = jnp.zeros((128, 1024), BF)
    convolve(2, 80, 0)
    convolve(2, 80, 1)
    for r in range(2):
        rows = acc[128 * r : 128 * r + 128]
        result = jnp.concatenate([rows[:, 0:256], rows[:, 320:384]], axis=1)
        out_ref[r] = ((result + vector(5) + sample[2 * h + r]).T).astype(BF)
    for copy in swaps + [lat_copy] + copies:
        copy.wait_send()


def shards(latents, mean_one, rstd_one, gain_one, shift_one, kernel_one, bias_one, embed_bias,
           mean_two, rstd_two, gain_two, shift_two, kernel_two, bias_two):
    lat = jnp.transpose(latents[0], (0, 2, 1))
    k1 = jnp.transpose(kernel_one, (1, 0, 2))
    k2 = jnp.transpose(kernel_two, (1, 0, 2))
    vmem = pl.BlockSpec(memory_space=pltpu.VMEM)
    pin = lambda v: pltpu.with_memory_space_constraint(v, pltpu.HBM)
    out = pl.pallas_call(
        kernel,
        out_shape=jax.ShapeDtypeStruct((2, 320, 128), BF),
        in_specs=[pl.BlockSpec(memory_space=pltpu.HBM)] * 14,
        out_specs=vmem,
        scratch_shapes=[
            pltpu.VMEM((2, 2, 320, 128), BF),
            pltpu.VMEM((2, 9, 4, 200), BF),
            pltpu.VMEM((8, 320), F32),
            pltpu.VMEM((4, 1, 32), F32),
            pltpu.VMEM((4, 2, 16, 256), BF),
            pltpu.VMEM((8, 2, 16, 256), BF),
            pltpu.VMEM((2, 2, 4, 8, SLOT, 128), BF),
            pltpu.VMEM((6, 128, 1024), BF),
            pltpu.VMEM((4, 128, 320), F32),
            pltpu.VMEM((320, 1024), BF),
            pltpu.VMEM((384, 384), F32),
            pltpu.SemaphoreType.DMA, pltpu.SemaphoreType.DMA,
            pltpu.SemaphoreType.DMA((7,)), pltpu.SemaphoreType.DMA((7,)),
            pltpu.SemaphoreType.DMA((COPIES,)), pltpu.SemaphoreType.DMA((COPIES,)),
            pltpu.SemaphoreType.DMA((14,)),
        ],
        compiler_params=pltpu.CompilerParams(
            collective_id=0, has_side_effects=True, vmem_limit_bytes=40 * 2**20),
        name="residual_block",
    )(*map(pin, (lat, mean_one, rstd_one, gain_one, shift_one, k1, bias_one, embed_bias,
      mean_two, rstd_two, gain_two, shift_two, k2, bias_two)))
    return jnp.transpose(out, (0, 2, 1))[None]


def solution(mesh):
    placed = (
        P("dp", "rows", None, None), P("dp", None), P("dp", None), P(), P(), P(None, None, "dp"), P(),
        P("dp", None), P("dp", None), P("dp", None), P(), P(), P(None, None, "dp"), P(),
    )
    return jax.shard_map(
        shards, mesh=mesh, in_specs=placed, out_specs=P("dp", "rows", None, None), check_vma=False
    )
```

```python
from functools import partial

import jax
import jax.numpy as jnp
from jax import lax
from jax.experimental import pallas as pl
from jax.experimental.pallas import tpu as pltpu
from jax.sharding import PartitionSpec as P

MESH = pl.DeviceIdType.MESH
BF = jnp.bfloat16
F32 = jnp.float32
REL = (0, 1, -1, 2, -2, 3, -3, 4)
CHUNKS = ((0, 1), (1, 3), (3, 5), (5, 8))
Z_ORDER = (1, 2, 3, 4, 5, 6, 7)
FAR = ()
COPIES = 64
SWAPS = tuple((a, b) for a in range(4) for b in range(2) if (a, b) != (0, 0))
SLOT = 128


def device(x, y, z, c):
    x, y, z, c = lax.rem(x + 4, 4), lax.rem(y + 4, 4), lax.rem(z + 8, 8), lax.rem(c + 2, 2)
    return (lax.rem(x, 2) * 64 + z * 8 + y * 2 + c, lax.div(x, 2))


def silu_norm(values, mean, rstd, gain, shift):
    scaled = ((values - mean) * rstd) * gain + shift
    return scaled / (1.0 + jnp.exp(-scaled))


def spread(channel_values):
    group = lax.broadcasted_iota(jnp.int32, (32, 320), 0)
    lane = lax.broadcasted_iota(jnp.int32, (32, 320), 1)
    pick = jnp.where(lane // 10 == group, 1.0, 0.0).astype(F32)
    wide = jnp.broadcast_to(channel_values, (8, 32))
    return jnp.dot(wide, pick, precision=lax.Precision.HIGHEST, preferred_element_type=F32)[0:1]


def expand(act, pick, tap_lane):
    wide = jnp.dot(act, pick, preferred_element_type=F32)
    row = lax.broadcasted_iota(jnp.int32, (128, 1024), 0)
    before = jnp.where(row == 0, 0.0, pltpu.roll(wide, 1, 0))
    after = jnp.where(row == 127, 0.0, pltpu.roll(wide, 127, 0))
    return jnp.where(tap_lane < 5, before, jnp.where(tap_lane < 10, wide, after)).astype(BF)


def distance(place):
    return ((place + 1) // 2) * (2 * (place % 2) - 1)


def kernel(
    lat_ref, mean1, rstd1, gain1, shift1, k1_ref, bias1, embed, mean2, rstd2, gain2, shift2, k2_ref, bias2,
    out_ref,
    lat, raw, vectors, stats, msg, got, held, lhs, sample, pick, acc,
    lat_send, lat_recv, swap_send, swap_recv, sent, landed, local_sem,
):
    d = lax.axis_index("dp")
    h = lax.axis_index("rows")
    c = d % 2
    y = (d // 2) % 4
    z = (d // 8) % 8
    xl = d // 64
    x = 2 * h + xl

    barrier = pltpu.get_barrier_semaphore()
    partners = [device(x, y - a, z, c - b) for a, b in SWAPS]
    partners += [device(x, y, z - s, c) for s in REL[1:]]
    partners += [device(x + s, y, z, c) for s in (1, 2, 3)]
    for partner in partners:
        pl.semaphore_signal(barrier, inc=1, device_id=partner, device_id_type=MESH)

    local = []
    for i, (source, target) in enumerate((
        (k1_ref, raw.at[0]), (k2_ref, raw.at[1]), (lat_ref, lat.at[h]),
        (mean1, stats.at[0]), (rstd1, stats.at[1]), (mean2, stats.at[2]), (rstd2, stats.at[3]),
        (gain1, vectors.at[0]), (shift1, vectors.at[1]), (bias1, vectors.at[2]),
        (gain2, vectors.at[3]), (shift2, vectors.at[4]), (bias2, vectors.at[5]), (embed, vectors.at[pl.ds(6, 1)]),
    )):
        copy = pltpu.make_async_copy(source, target, local_sem.at[i])
        copy.start()
        local.append(copy)

    msg[...] = jnp.zeros_like(msg)
    for number in range(2):
        local[number].wait()
        block = raw[number].astype(F32)
        for b in range(4):
            msg[b, number, 0:9, 0:200] = block[:, b, :].astype(BF)

    pl.semaphore_wait(barrier, len(partners))

    swaps = []
    q = 2 * y + c
    for i, (a, b) in enumerate(SWAPS):
        copy = pltpu.make_async_remote_copy(
            src_ref=msg.at[(y + a + 2 * h) % 4], dst_ref=got.at[q], send_sem=swap_send.at[i], recv_sem=swap_recv.at[i],
            device_id=device(x, y + a, z, c + b), device_id_type=MESH)
        copy.start()
        swaps.append(copy)
    lat_copy = pltpu.make_async_remote_copy(
        src_ref=lat_ref, dst_ref=lat.at[h], send_sem=lat_send, recv_sem=lat_recv,
        device_id=device(x + 2, y, z, c), device_id_type=MESH)
    lat_copy.start()
    got[q] = msg[(y + 2 * h) % 4]

    lane = lax.broadcasted_iota(jnp.int32, (1, 1024), 1)
    within = lane % 16
    group = lane // 16
    zz = (z + distance(group % 8) + 8) % 8
    side = group // 32
    row = (group // 8) % 4
    bb = (y + jnp.where(side == 0, distance(row) + 2 * h, row) + 4) % 4
    xx = (xl + side) % 2
    wanted = jnp.where(within < 15, bb * 80 + (xx * 8 + zz) * 5 + within % 5, -1)
    channel = lax.broadcasted_iota(jnp.int32, (320, 1024), 0)
    pick[...] = jnp.where(wanted == channel, 1.0, 0.0).astype(BF)

    tap_lane = lax.broadcasted_iota(jnp.int32, (128, 1024), 1) % 16

    def vector(i):
        return vectors[i : i + 1]

    for copy in local[2:]:
        copy.wait()
    m1, r1 = spread(stats[0]), spread(stats[1])
    m2, r2 = spread(stats[2]), spread(stats[3])
    lhs[0] = jnp.zeros((128, 1024), BF)
    lhs[5] = jnp.zeros((128, 1024), BF)

    def activate(half, r):
        values = lat[half, r].astype(F32).T
        sample[2 * half + r] = values
        lhs[2 * half + r + 1] = expand(
            silu_norm(values, m1, r1, vector(0), vector(1)).astype(BF), pick[...], tap_lane)

    activate(h, 0)
    activate(h, 1)

    for copy in swaps:
        copy.wait_recv()

    col = lax.broadcasted_iota(jnp.int32, (16, 384), 1)
    row48 = lax.broadcasted_iota(jnp.int32, (48, 80), 0)
    col80 = lax.broadcasted_iota(jnp.int32, (48, 80), 1)
    in_tile = row48 % 16
    source = (in_tile % 5) * 16 + (row48 // 16) * 3 + in_tile // 5
    place = jnp.where((source == col80) & (in_tile < 15), 1.0, 0.0).astype(BF)
    whole = []
    for number in range(2):
        pieces = [
            jnp.concatenate([got[i, number].astype(F32), jnp.zeros((16, 128), F32)], axis=1) for i in range(8)
        ]
        rows = []
        for p in range(5):
            total = jnp.zeros((16, 384), F32)
            for i in range(8):
                by = 200 * i - 320 * p
                low, high = max(0, -by), min(200, 320 - by)
                if low < high:
                    part = jnp.where((col >= low) & (col < high), pieces[i], 0.0)
                    total = total + (pltpu.roll(part, by % 384, 1) if by % 384 else part)
            rows.append(total)
        stacked = jnp.concatenate(rows, axis=0).astype(BF)
        whole.append(jnp.dot(place, stacked, preferred_element_type=F32))
    one, two = whole
    first = c == 0
    own = held.at[0, 0, 0, 0]
    own[0:48] = jnp.where(first, one[:, 0:128], one[:, 128:256]).astype(BF)
    own[80:128] = jnp.where(first, two[:, 0:128], two[:, 128:256]).astype(BF)
    last = one[:, 256:384] + pltpu.roll(two[:, 256:384], 64, 1)
    own[48:80] = jnp.where(first, last[0:32], last[16:48]).astype(BF)

    up, down, far = device(x, y + 1, z, c), device(x, y - 1, z, c), device(x, y + 2, z, c)
    right, left, sibling = device(x + 1, y, z, c), device(x - 1, y, z, c), device(x, y, z, c + 1)
    copies = []
    count = [0]

    def send(source, target, to, recv=None):
        i = len(copies)
        if recv is None:
            recv = landed.at[count[0]]
            count[0] += 1
        copy = pltpu.make_async_remote_copy(
            src_ref=source, dst_ref=target, send_sem=sent.at[i], recv_sem=recv, device_id=to, device_id_type=MESH)
        copy.start()
        copies.append(copy)
        return copy

    def at(xr, yr, chunk, core=0):
        low, high = chunk
        return held.at[core, xr, yr, pl.ds(low, high - low)]

    z_copies, y_copies, far_copies, x_copies, core_copies = {}, {}, {}, {}, ({}, {})

    def send_z():
        for i in Z_ORDER:
            back = REL.index(-REL[i]) if REL[i] != 4 else 7
            z_copies[back] = send(at(0, 0, (0, 1)), at(0, 0, (back, back + 1)), device(x, y, z + REL[i], c))

    def send_x(k, j):
        base = count[0]
        count[0] += 2
        for to in (right, left):
            send(at(0, j, CHUNKS[k]), at(1, 2 * h + j, CHUNKS[k]), to, landed.at[base + h])
        x_copies.setdefault(k, []).append(base)

    def send_core(k, xr):
        ys = pl.ds(0, 4)
        core_copies[xr][k] = send(at(xr, ys, CHUNKS[k]), at(xr, ys, CHUNKS[k], 1), sibling)

    def after_z(k):
        chunk = CHUNKS[k]
        for i in range(*chunk):
            if i:
                z_copies[i].wait_recv()
        y_copies[k] = send(at(0, 0, chunk), at(0, 1, chunk), down), send(at(0, 0, chunk), at(0, 2, chunk), up)
        if k in FAR:
            far_copies[k] = send(at(0, 0, chunk), at(0, 3, chunk), far)
        send_x(k, 0)

    def after_y(k):
        chunk = CHUNKS[k]
        from_up, from_down = y_copies[k]
        from_up.wait_recv()
        if k % 2 and k not in FAR:
            far_copies[k] = send(at(0, 1, chunk), at(0, 3, chunk), down)
        send_x(k, 1)
        from_down.wait_recv()
        if k % 2 == 0 and k not in FAR:
            far_copies[k] = send(at(0, 2, chunk), at(0, 3, chunk), up)

    def after_far(k):
        far_copies[k].wait_recv()
        send_core(k, 0)

    def after_x(k):
        for base in x_copies[k]:
            for side in range(2):
                ref = at(1, 0, CHUNKS[k])
                pltpu.make_async_remote_copy(
                    src_ref=ref, dst_ref=ref, send_sem=sent.at[0], recv_sem=landed.at[base + side],
                    device_id=right, device_id_type=MESH).wait_recv()
        send_core(k, 1)

    send_z()
    after_z(0)
    lat_copy.wait_recv()
    activate(1 - h, 0)
    after_z(1)
    after_y(0)
    activate(1 - h, 1)
    after_z(2)
    after_y(1)
    after_z(3)
    after_y(2)
    after_far(0)
    after_far(1)
    after_y(3)
    after_x(0)
    after_x(1)
    after_far(2)
    after_x(2)
    after_far(3)
    after_x(3)

    def weights(dy, base, half):
        t0 = held[c, half, :, :, base + 16 * dy : base + 16 * dy + 16].reshape(512, 128)
        t1 = held[1 - c, half, :, :, base + 16 * dy : base + 16 * dy + 16].reshape(512, 128)
        owner, row = ((c, 48), (c, 64), (1 - c, 64))[dy]
        t2 = held[owner, half, :, :, row : row + 16].reshape(512, 128)
        return jnp.concatenate([t0, t1, t2], axis=1)

    def convolve(rows, base, half):
        for dy in range(3):
            left_side = lhs[pl.ds(h + dy, rows), :, 512 * half : 512 * half + 512].reshape(128 * rows, 512)
            product = jnp.dot(left_side, weights(dy, base, half), preferred_element_type=F32)
            if dy or half:
                acc[0 : 128 * rows] += product
            else:
                acc[0 : 128 * rows] = product

    for copy in core_copies[0].values():
        copy.wait_recv()
    convolve(3, 0, 0)
    for copy in core_copies[1].values():
        copy.wait_recv()
    convolve(3, 0, 1)

    offset = vector(2) + vector(6)
    for r in range(3):
        hidden = acc[128 * r : 128 * r + 128, 0:320] + offset
        lhs[r + 1] = expand(silu_norm(hidden, m2, r2, vector(3), vector(4)).astype(BF), pick[...], tap_lane)
    lhs[4] = jnp.zeros((128, 1024), BF)
    convolve(2, 80, 0)
    convolve(2, 80, 1)
    for r in range(2):
        rows = acc[128 * r : 128 * r + 128]
        result = jnp.concatenate([rows[:, 0:256], rows[:, 320:384]], axis=1)
        out_ref[r] = ((result + vector(5) + sample[2 * h + r]).T).astype(BF)
    for copy in swaps + [lat_copy] + copies:
        copy.wait_send()


def shards(latents, mean_one, rstd_one, gain_one, shift_one, kernel_one, bias_one, embed_bias,
           mean_two, rstd_two, gain_two, shift_two, kernel_two, bias_two):
    lat = jnp.transpose(latents[0], (0, 2, 1))
    k1 = jnp.transpose(kernel_one, (1, 0, 2))
    k2 = jnp.transpose(kernel_two, (1, 0, 2))
    vmem = pl.BlockSpec(memory_space=pltpu.VMEM)
    pin = lambda v: pltpu.with_memory_space_constraint(v, pltpu.HBM)
    out = pl.pallas_call(
        kernel,
        out_shape=jax.ShapeDtypeStruct((2, 320, 128), BF),
        in_specs=[pl.BlockSpec(memory_space=pltpu.HBM)] * 14,
        out_specs=vmem,
        scratch_shapes=[
            pltpu.VMEM((2, 2, 320, 128), BF),
            pltpu.VMEM((2, 9, 4, 200), BF),
            pltpu.VMEM((8, 320), F32),
            pltpu.VMEM((4, 1, 32), F32),
            pltpu.VMEM((4, 2, 16, 256), BF),
            pltpu.VMEM((8, 2, 16, 256), BF),
            pltpu.VMEM((2, 2, 4, 8, SLOT, 128), BF),
            pltpu.VMEM((6, 128, 1024), BF),
            pltpu.VMEM((4, 128, 320), F32),
            pltpu.VMEM((320, 1024), BF),
            pltpu.VMEM((384, 384), F32),
            pltpu.SemaphoreType.DMA, pltpu.SemaphoreType.DMA,
            pltpu.SemaphoreType.DMA((7,)), pltpu.SemaphoreType.DMA((7,)),
            pltpu.SemaphoreType.DMA((COPIES,)), pltpu.SemaphoreType.DMA((COPIES,)),
            pltpu.SemaphoreType.DMA((14,)),
        ],
        compiler_params=pltpu.CompilerParams(
            collective_id=0, has_side_effects=True, vmem_limit_bytes=40 * 2**20),
        name="residual_block",
    )(*map(pin, (lat, mean_one, rstd_one, gain_one, shift_one, k1, bias_one, embed_bias,
      mean_two, rstd_two, gain_two, shift_two, k2, bias_two)))
    return jnp.transpose(out, (0, 2, 1))[None]


def solution(mesh):
    placed = (
        P("dp", "rows", None, None), P("dp", None), P("dp", None), P(), P(), P(None, None, "dp"), P(),
        P("dp", None), P("dp", None), P("dp", None), P(), P(), P(None, None, "dp"), P(),
    )
    return jax.shard_map(
        shards, mesh=mesh, in_specs=placed, out_specs=P("dp", "rows", None, None), check_vma=False
    )
```

```python
from functools import partial

import jax
import jax.numpy as jnp
from jax import lax
from jax.experimental import pallas as pl
from jax.experimental.pallas import tpu as pltpu
from jax.sharding import PartitionSpec as P

MESH = pl.DeviceIdType.MESH
BF = jnp.bfloat16
F32 = jnp.float32
REL = (0, 1, -1, 2, -2, 3, -3, 4)
CHUNKS = ((0, 1), (1, 3), (3, 5), (5, 8))
Z_ORDER = (1, 2, 3, 4, 5, 6, 7)
FAR = (0,)
ACROSS = (1,)
TURNED = (1, 2, 3)
COPIES = 64
SWAPS = tuple((a, b) for a in range(4) for b in range(2) if (a, b) != (0, 0))
SLOT = 128


def device(x, y, z, c):
    x, y, z, c = lax.rem(x + 4, 4), lax.rem(y + 4, 4), lax.rem(z + 8, 8), lax.rem(c + 2, 2)
    return (lax.rem(x, 2) * 64 + z * 8 + y * 2 + c, lax.div(x, 2))


def silu_norm(values, mean, rstd, gain, shift):
    scaled = ((values - mean) * rstd) * gain + shift
    return scaled / (1.0 + jnp.exp(-scaled))


def spread(channel_values):
    group = lax.broadcasted_iota(jnp.int32, (32, 320), 0)
    lane = lax.broadcasted_iota(jnp.int32, (32, 320), 1)
    pick = jnp.where(lane // 10 == group, 1.0, 0.0).astype(F32)
    wide = jnp.broadcast_to(channel_values, (8, 32))
    return jnp.dot(wide, pick, precision=lax.Precision.HIGHEST, preferred_element_type=F32)[0:1]


def expand(act, pick, tap_lane):
    wide = jnp.dot(act, pick, preferred_element_type=F32)
    row = lax.broadcasted_iota(jnp.int32, (128, 1024), 0)
    before = jnp.where(row == 0, 0.0, pltpu.roll(wide, 1, 0))
    after = jnp.where(row == 127, 0.0, pltpu.roll(wide, 127, 0))
    return jnp.where(tap_lane < 5, before, jnp.where(tap_lane < 10, wide, after)).astype(BF)


def distance(place):
    return ((place + 1) // 2) * (2 * (place % 2) - 1)


def kernel(
    lat_ref, mean1, rstd1, gain1, shift1, k1_ref, bias1, embed, mean2, rstd2, gain2, shift2, k2_ref, bias2,
    out_ref,
    lat, raw, vectors, stats, msg, got, held, lhs, sample, pick, acc,
    lat_send, lat_recv, swap_send, swap_recv, sent, landed, local_sem,
):
    d = lax.axis_index("dp")
    h = lax.axis_index("rows")
    c = d % 2
    y = (d // 2) % 4
    z = (d // 8) % 8
    xl = d // 64
    x = 2 * h + xl

    barrier = pltpu.get_barrier_semaphore()
    partners = [device(x, y - a, z, c - b) for a, b in SWAPS]
    partners += [device(x, y, z - s, c) for s in REL[1:]]
    partners += [device(x + s, y, z, c) for s in (1, 2, 3)]
    for partner in partners:
        pl.semaphore_signal(barrier, inc=1, device_id=partner, device_id_type=MESH)

    local = []
    for i, (source, target) in enumerate((
        (k1_ref, raw.at[0]), (k2_ref, raw.at[1]), (lat_ref, lat.at[h]),
        (mean1, stats.at[0]), (rstd1, stats.at[1]), (mean2, stats.at[2]), (rstd2, stats.at[3]),
        (gain1, vectors.at[0]), (shift1, vectors.at[1]), (bias1, vectors.at[2]),
        (gain2, vectors.at[3]), (shift2, vectors.at[4]), (bias2, vectors.at[5]), (embed, vectors.at[pl.ds(6, 1)]),
    )):
        copy = pltpu.make_async_copy(source, target, local_sem.at[i])
        copy.start()
        local.append(copy)

    msg[...] = jnp.zeros_like(msg)
    for number in range(2):
        local[number].wait()
        block = raw[number].astype(F32)
        for b in range(4):
            msg[b, number, 0:9, 0:200] = block[:, b, :].astype(BF)

    pl.semaphore_wait(barrier, len(partners))

    swaps = []
    q = 2 * y + c
    for i, (a, b) in enumerate(SWAPS):
        copy = pltpu.make_async_remote_copy(
            src_ref=msg.at[(y + a + 2 * h) % 4], dst_ref=got.at[q], send_sem=swap_send.at[i], recv_sem=swap_recv.at[i],
            device_id=device(x, y + a, z, c + b), device_id_type=MESH)
        copy.start()
        swaps.append(copy)
    lat_copy = pltpu.make_async_remote_copy(
        src_ref=lat_ref, dst_ref=lat.at[h], send_sem=lat_send, recv_sem=lat_recv,
        device_id=device(x + 2, y, z, c), device_id_type=MESH)
    lat_copy.start()
    got[q] = msg[(y + 2 * h) % 4]

    lane = lax.broadcasted_iota(jnp.int32, (1, 1024), 1)
    within = lane % 16
    group = lane // 16
    zz = (z + distance(group % 8) + 8) % 8
    side = group // 32
    row = (group // 8) % 4
    bb = (y + jnp.where(side == 0, distance(row) + 2 * h, row) + 4) % 4
    xx = (xl + side) % 2
    wanted = jnp.where(within < 15, bb * 80 + (xx * 8 + zz) * 5 + within % 5, -1)
    channel = lax.broadcasted_iota(jnp.int32, (320, 1024), 0)
    pick[...] = jnp.where(wanted == channel, 1.0, 0.0).astype(BF)

    tap_lane = lax.broadcasted_iota(jnp.int32, (128, 1024), 1) % 16

    def vector(i):
        return vectors[i : i + 1]

    for copy in local[2:]:
        copy.wait()
    m1, r1 = spread(stats[0]), spread(stats[1])
    m2, r2 = spread(stats[2]), spread(stats[3])
    lhs[0] = jnp.zeros((128, 1024), BF)
    lhs[5] = jnp.zeros((128, 1024), BF)

    def activate(half, r):
        values = lat[half, r].astype(F32).T
        sample[2 * half + r] = values
        lhs[2 * half + r + 1] = expand(
            silu_norm(values, m1, r1, vector(0), vector(1)).astype(BF), pick[...], tap_lane)

    activate(h, 0)
    activate(h, 1)

    for copy in swaps:
        copy.wait_recv()

    col = lax.broadcasted_iota(jnp.int32, (16, 384), 1)
    row48 = lax.broadcasted_iota(jnp.int32, (48, 80), 0)
    col80 = lax.broadcasted_iota(jnp.int32, (48, 80), 1)
    in_tile = row48 % 16
    source = (in_tile % 5) * 16 + (row48 // 16) * 3 + in_tile // 5
    place = jnp.where((source == col80) & (in_tile < 15), 1.0, 0.0).astype(BF)
    whole = []
    for number in range(2):
        pieces = [
            jnp.concatenate([got[i, number].astype(F32), jnp.zeros((16, 128), F32)], axis=1) for i in range(8)
        ]
        rows = []
        for p in range(5):
            total = jnp.zeros((16, 384), F32)
            for i in range(8):
                by = 200 * i - 320 * p
                low, high = max(0, -by), min(200, 320 - by)
                if low < high:
                    part = jnp.where((col >= low) & (col < high), pieces[i], 0.0)
                    total = total + (pltpu.roll(part, by % 384, 1) if by % 384 else part)
            rows.append(total)
        stacked = jnp.concatenate(rows, axis=0).astype(BF)
        whole.append(jnp.dot(place, stacked, preferred_element_type=F32))
    one, two = whole
    first = c == 0
    own = held.at[0, 0, 0, 0]
    own[0:48] = jnp.where(first, one[:, 0:128], one[:, 128:256]).astype(BF)
    own[80:128] = jnp.where(first, two[:, 0:128], two[:, 128:256]).astype(BF)
    last = one[:, 256:384] + pltpu.roll(two[:, 256:384], 64, 1)
    own[48:80] = jnp.where(first, last[0:32], last[16:48]).astype(BF)

    up, down, far = device(x, y + 1, z, c), device(x, y - 1, z, c), device(x, y + 2, z, c)
    right, left, sibling = device(x + 1, y, z, c), device(x - 1, y, z, c), device(x, y, z, c + 1)
    copies = []
    count = [0]

    def send(source, target, to, recv=None):
        i = len(copies)
        if recv is None:
            recv = landed.at[count[0]]
            count[0] += 1
        copy = pltpu.make_async_remote_copy(
            src_ref=source, dst_ref=target, send_sem=sent.at[i], recv_sem=recv, device_id=to, device_id_type=MESH)
        copy.start()
        copies.append(copy)
        return copy

    def at(xr, yr, chunk, core=0):
        low, high = chunk
        return held.at[core, xr, yr, pl.ds(low, high - low)]

    turned = {}
    z_copies, y_copies, far_copies, x_copies, core_copies = {}, {}, {}, {}, ({}, {})

    def send_z():
        for i in Z_ORDER:
            back = REL.index(-REL[i]) if REL[i] != 4 else 7
            z_copies[back] = send(at(0, 0, (0, 1)), at(0, 0, (back, back + 1)), device(x, y, z + REL[i], c))

    def send_x(k, j):
        base = count[0]
        count[0] += 2
        for to in (right, left):
            send(at(0, j, CHUNKS[k]), at(1, 2 * h + j, CHUNKS[k]), to, landed.at[base + h])
        x_copies.setdefault(k, []).append(base)

    def send_core(k, xr):
        ys = pl.ds(0, 4)
        core_copies[xr][k] = send(at(xr, ys, CHUNKS[k]), at(xr, ys, CHUNKS[k], 1), sibling)

    def after_z(k):
        chunk = CHUNKS[k]
        for i in range(*chunk):
            if i:
                z_copies[i].wait_recv()
        y_copies[k] = send(at(0, 0, chunk), at(0, 1, chunk), down), send(at(0, 0, chunk), at(0, 2, chunk), up)
        if k in FAR:
            far_copies[k] = send(at(0, 0, chunk), at(0, 3, chunk), far)
        send_x(k, 0)

    def after_y(k):
        chunk = CHUNKS[k]
        from_up, from_down = y_copies[k]
        from_up.wait_recv()
        if k % 2 and k not in FAR + TURNED:
            far_copies[k] = send(at(0, 1, chunk), at(0, 3, chunk), down)
        if k not in ACROSS:
            send_x(k, 1)
        from_down.wait_recv()
        if k % 2 == 0 and k not in FAR + TURNED:
            far_copies[k] = send(at(0, 2, chunk), at(0, 3, chunk), up)

    def turn():
        for i in Z_ORDER:
            back = REL.index(-REL[i]) if REL[i] != 4 else 7
            if any(CHUNKS[k][0] <= back < CHUNKS[k][1] for k in TURNED):
                turned[back] = send(at(0, 3, (0, 1)), at(0, 3, (back, back + 1)), device(x, y, z + REL[i], c))

    def after_far(k):
        if k in TURNED:
            for i in range(*CHUNKS[k]):
                turned[i].wait_recv()
        else:
            far_copies[k].wait_recv()
        if k == 0:
            turn()
        send_core(k, 0)

    def wait_x(k, base):
        for side in range(2):
            ref = at(1, 0, CHUNKS[k])
            pltpu.make_async_remote_copy(
                src_ref=ref, dst_ref=ref, send_sem=sent.at[0], recv_sem=landed.at[base + side],
                device_id=right, device_id_type=MESH).wait_recv()

    crossed = {}

    def cross(k):
        chunk = CHUNKS[k]
        wait_x(k, x_copies[k][0])
        crossed[k] = send(at(1, 0, chunk), at(1, 1, chunk), down), send(at(1, 0, chunk), at(1, 3, chunk), up)

    def after_x(k):
        if k in ACROSS:
            for copy in crossed[k]:
                copy.wait_recv()
        else:
            for base in x_copies[k]:
                wait_x(k, base)
        send_core(k, 1)

    send_z()
    after_z(0)
    lat_copy.wait_recv()
    activate(1 - h, 0)
    after_z(1)
    after_y(0)
    after_far(0)
    activate(1 - h, 1)
    after_z(2)
    after_y(1)
    after_z(3)
    cross(1)
    after_y(2)
    after_far(1)
    after_x(0)
    after_y(3)
    after_x(1)
    after_far(2)
    after_x(2)
    after_far(3)
    after_x(3)

    def weights(dy, base, half):
        t0 = held[c, half, :, :, base + 16 * dy : base + 16 * dy + 16].reshape(512, 128)
        t1 = held[1 - c, half, :, :, base + 16 * dy : base + 16 * dy + 16].reshape(512, 128)
        owner, row = ((c, 48), (c, 64), (1 - c, 64))[dy]
        t2 = held[owner, half, :, :, row : row + 16].reshape(512, 128)
        return jnp.concatenate([t0, t1, t2], axis=1)

    def convolve(rows, base, half):
        for dy in range(3):
            left_side = lhs[pl.ds(h + dy, rows), :, 512 * half : 512 * half + 512].reshape(128 * rows, 512)
            product = jnp.dot(left_side, weights(dy, base, half), preferred_element_type=F32)
            if dy or half:
                acc[0 : 128 * rows] += product
            else:
                acc[0 : 128 * rows] = product

    for copy in core_copies[0].values():
        copy.wait_recv()
    convolve(3, 0, 0)
    for copy in core_copies[1].values():
        copy.wait_recv()
    convolve(3, 0, 1)

    offset = vector(2) + vector(6)
    for r in range(3):
        hidden = acc[128 * r : 128 * r + 128, 0:320] + offset
        lhs[r + 1] = expand(silu_norm(hidden, m2, r2, vector(3), vector(4)).astype(BF), pick[...], tap_lane)
    lhs[4] = jnp.zeros((128, 1024), BF)
    convolve(2, 80, 0)
    convolve(2, 80, 1)
    for r in range(2):
        rows = acc[128 * r : 128 * r + 128]
        result = jnp.concatenate([rows[:, 0:256], rows[:, 320:384]], axis=1)
        out_ref[r] = ((result + vector(5) + sample[2 * h + r]).T).astype(BF)
    for copy in swaps + [lat_copy] + copies:
        copy.wait_send()


def shards(latents, mean_one, rstd_one, gain_one, shift_one, kernel_one, bias_one, embed_bias,
           mean_two, rstd_two, gain_two, shift_two, kernel_two, bias_two):
    lat = jnp.transpose(latents[0], (0, 2, 1))
    k1 = jnp.transpose(kernel_one, (1, 0, 2))
    k2 = jnp.transpose(kernel_two, (1, 0, 2))
    vmem = pl.BlockSpec(memory_space=pltpu.VMEM)
    pin = lambda v: pltpu.with_memory_space_constraint(v, pltpu.HBM)
    out = pl.pallas_call(
        kernel,
        out_shape=jax.ShapeDtypeStruct((2, 320, 128), BF),
        in_specs=[pl.BlockSpec(memory_space=pltpu.HBM)] * 14,
        out_specs=vmem,
        scratch_shapes=[
            pltpu.VMEM((2, 2, 320, 128), BF),
            pltpu.VMEM((2, 9, 4, 200), BF),
            pltpu.VMEM((8, 320), F32),
            pltpu.VMEM((4, 1, 32), F32),
            pltpu.VMEM((4, 2, 16, 256), BF),
            pltpu.VMEM((8, 2, 16, 256), BF),
            pltpu.VMEM((2, 2, 4, 8, SLOT, 128), BF),
            pltpu.VMEM((6, 128, 1024), BF),
            pltpu.VMEM((4, 128, 320), F32),
            pltpu.VMEM((320, 1024), BF),
            pltpu.VMEM((384, 384), F32),
            pltpu.SemaphoreType.DMA, pltpu.SemaphoreType.DMA,
            pltpu.SemaphoreType.DMA((7,)), pltpu.SemaphoreType.DMA((7,)),
            pltpu.SemaphoreType.DMA((COPIES,)), pltpu.SemaphoreType.DMA((COPIES,)),
            pltpu.SemaphoreType.DMA((14,)),
        ],
        compiler_params=pltpu.CompilerParams(
            collective_id=0, has_side_effects=True, vmem_limit_bytes=40 * 2**20),
        name="residual_block",
    )(*map(pin, (lat, mean_one, rstd_one, gain_one, shift_one, k1, bias_one, embed_bias,
      mean_two, rstd_two, gain_two, shift_two, k2, bias_two)))
    return jnp.transpose(out, (0, 2, 1))[None]


def solution(mesh):
    placed = (
        P("dp", "rows", None, None), P("dp", None), P("dp", None), P(), P(), P(None, None, "dp"), P(),
        P("dp", None), P("dp", None), P("dp", None), P(), P(), P(None, None, "dp"), P(),
    )
    return jax.shard_map(
        shards, mesh=mesh, in_specs=placed, out_specs=P("dp", "rows", None, None), check_vma=False
    )
```

```python
from functools import partial

import jax
import jax.numpy as jnp
from jax import lax
from jax.experimental import pallas as pl
from jax.experimental.pallas import tpu as pltpu
from jax.sharding import PartitionSpec as P

MESH = pl.DeviceIdType.MESH
BF = jnp.bfloat16
F32 = jnp.float32
REL = (0, 1, -1, 2, -2, 3, -3, 4)
CHUNKS = ((0, 1), (1, 3), (3, 5), (5, 8))
Z_ORDER = (1, 2, 3, 4, 5, 6, 7)
FAR = (0,)
ACROSS = (1,)
TURNED = (1, 2, 3)
COPIES = 64
SWAPS = tuple((a, b) for a in range(4) for b in range(2) if (a, b) != (0, 0))
SLOT = 128


def device(x, y, z, c):
    x, y, z, c = lax.rem(x + 4, 4), lax.rem(y + 4, 4), lax.rem(z + 8, 8), lax.rem(c + 2, 2)
    return (lax.rem(x, 2) * 64 + z * 8 + y * 2 + c, lax.div(x, 2))


def silu_norm(values, mean, rstd, gain, shift):
    scaled = ((values - mean) * rstd) * gain + shift
    return scaled / (1.0 + jnp.exp(-scaled))


def spread(channel_values):
    group = lax.broadcasted_iota(jnp.int32, (32, 320), 0)
    lane = lax.broadcasted_iota(jnp.int32, (32, 320), 1)
    pick = jnp.where(lane // 10 == group, 1.0, 0.0).astype(F32)
    wide = jnp.broadcast_to(channel_values, (8, 32))
    return jnp.dot(wide, pick, precision=lax.Precision.HIGHEST, preferred_element_type=F32)[0:1]


def expand(act, pick, tap_lane):
    wide = jnp.dot(act, pick, preferred_element_type=F32)
    row = lax.broadcasted_iota(jnp.int32, (128, 1024), 0)
    before = jnp.where(row == 0, 0.0, pltpu.roll(wide, 1, 0))
    after = jnp.where(row == 127, 0.0, pltpu.roll(wide, 127, 0))
    return jnp.where(tap_lane < 5, before, jnp.where(tap_lane < 10, wide, after)).astype(BF)


def distance(place):
    return ((place + 1) // 2) * (2 * (place % 2) - 1)


def kernel(
    lat_ref, mean1, rstd1, gain1, shift1, k1_ref, bias1, embed, mean2, rstd2, gain2, shift2, k2_ref, bias2,
    out_ref,
    lat, raw, vectors, stats, msg, got, held, lhs, sample, pick, acc,
    lat_send, lat_recv, swap_send, swap_recv, sent, landed, local_sem,
):
    d = lax.axis_index("dp")
    h = lax.axis_index("rows")
    c = d % 2
    y = (d // 2) % 4
    z = (d // 8) % 8
    xl = d // 64
    x = 2 * h + xl

    barrier = pltpu.get_barrier_semaphore()
    partners = [device(x, y - a, z, c - b) for a, b in SWAPS]
    partners += [device(x, y, z - s, c) for s in REL[1:]]
    partners += [device(x + s, y, z, c) for s in (1, 2, 3)]
    for partner in partners:
        pl.semaphore_signal(barrier, inc=1, device_id=partner, device_id_type=MESH)

    local = []
    for i, (source, target) in enumerate((
        (k1_ref, raw.at[0]), (k2_ref, raw.at[1]), (lat_ref, lat.at[h]),
        (mean1, stats.at[0]), (rstd1, stats.at[1]), (mean2, stats.at[2]), (rstd2, stats.at[3]),
        (gain1, vectors.at[0]), (shift1, vectors.at[1]), (bias1, vectors.at[2]),
        (gain2, vectors.at[3]), (shift2, vectors.at[4]), (bias2, vectors.at[5]), (embed, vectors.at[pl.ds(6, 1)]),
    )):
        copy = pltpu.make_async_copy(source, target, local_sem.at[i])
        copy.start()
        local.append(copy)

    msg[...] = jnp.zeros_like(msg)
    for number in range(2):
        local[number].wait()
        block = raw[number].astype(F32)
        for b in range(4):
            msg[b, number, 0:9, 0:200] = block[:, b, :].astype(BF)

    pl.semaphore_wait(barrier, len(partners))

    lat_copy = pltpu.make_async_remote_copy(
        src_ref=lat_ref, dst_ref=lat.at[h], send_sem=lat_send, recv_sem=lat_recv,
        device_id=device(x + 2, y, z, c), device_id_type=MESH)
    lat_copy.start()
    swaps = []
    q = 2 * y + c
    for i, (a, b) in enumerate(SWAPS):
        copy = pltpu.make_async_remote_copy(
            src_ref=msg.at[(y + a + 2 * h) % 4], dst_ref=got.at[q], send_sem=swap_send.at[i], recv_sem=swap_recv.at[i],
            device_id=device(x, y + a, z, c + b), device_id_type=MESH)
        copy.start()
        swaps.append(copy)
    got[q] = msg[(y + 2 * h) % 4]

    lane = lax.broadcasted_iota(jnp.int32, (1, 1024), 1)
    within = lane % 16
    group = lane // 16
    zz = (z + distance(group % 8) + 8) % 8
    side = group // 32
    row = (group // 8) % 4
    bb = (y + jnp.where(side == 0, distance(row) + 2 * h, row) + 4) % 4
    xx = (xl + side) % 2
    wanted = jnp.where(within < 15, bb * 80 + (xx * 8 + zz) * 5 + within % 5, -1)
    channel = lax.broadcasted_iota(jnp.int32, (320, 1024), 0)
    pick[...] = jnp.where(wanted == channel, 1.0, 0.0).astype(BF)

    tap_lane = lax.broadcasted_iota(jnp.int32, (128, 1024), 1) % 16

    def vector(i):
        return vectors[i : i + 1]

    for copy in local[2:]:
        copy.wait()
    m1, r1 = spread(stats[0]), spread(stats[1])
    m2, r2 = spread(stats[2]), spread(stats[3])
    lhs[0] = jnp.zeros((128, 1024), BF)
    lhs[5] = jnp.zeros((128, 1024), BF)

    def activate(half, r):
        values = lat[half, r].astype(F32).T
        sample[2 * half + r] = values
        lhs[2 * half + r + 1] = expand(
            silu_norm(values, m1, r1, vector(0), vector(1)).astype(BF), pick[...], tap_lane)

    activate(h, 0)
    activate(h, 1)

    for copy in swaps:
        copy.wait_recv()

    col = lax.broadcasted_iota(jnp.int32, (16, 384), 1)
    row48 = lax.broadcasted_iota(jnp.int32, (48, 80), 0)
    col80 = lax.broadcasted_iota(jnp.int32, (48, 80), 1)
    in_tile = row48 % 16
    source = (in_tile % 5) * 16 + (row48 // 16) * 3 + in_tile // 5
    place = jnp.where((source == col80) & (in_tile < 15), 1.0, 0.0).astype(BF)
    whole = []
    for number in range(2):
        pieces = [
            jnp.concatenate([got[i, number].astype(F32), jnp.zeros((16, 128), F32)], axis=1) for i in range(8)
        ]
        rows = []
        for p in range(5):
            total = jnp.zeros((16, 384), F32)
            for i in range(8):
                by = 200 * i - 320 * p
                low, high = max(0, -by), min(200, 320 - by)
                if low < high:
                    part = jnp.where((col >= low) & (col < high), pieces[i], 0.0)
                    total = total + (pltpu.roll(part, by % 384, 1) if by % 384 else part)
            rows.append(total)
        stacked = jnp.concatenate(rows, axis=0).astype(BF)
        whole.append(jnp.dot(place, stacked, preferred_element_type=F32))
    one, two = whole
    first = c == 0
    own = held.at[0, 0, 0, 0]
    own[0:48] = jnp.where(first, one[:, 0:128], one[:, 128:256]).astype(BF)
    own[80:128] = jnp.where(first, two[:, 0:128], two[:, 128:256]).astype(BF)
    last = one[:, 256:384] + pltpu.roll(two[:, 256:384], 64, 1)
    own[48:80] = jnp.where(first, last[0:32], last[16:48]).astype(BF)

    up, down, far = device(x, y + 1, z, c), device(x, y - 1, z, c), device(x, y + 2, z, c)
    right, left, sibling = device(x + 1, y, z, c), device(x - 1, y, z, c), device(x, y, z, c + 1)
    copies = []
    count = [0]

    def send(source, target, to, recv=None):
        i = len(copies)
        if recv is None:
            recv = landed.at[count[0]]
            count[0] += 1
        copy = pltpu.make_async_remote_copy(
            src_ref=source, dst_ref=target, send_sem=sent.at[i], recv_sem=recv, device_id=to, device_id_type=MESH)
        copy.start()
        copies.append(copy)
        return copy

    def at(xr, yr, chunk, core=0):
        low, high = chunk
        return held.at[core, xr, yr, pl.ds(low, high - low)]

    turned = {}
    z_copies, y_copies, far_copies, x_copies, core_copies = {}, {}, {}, {}, ({}, {})

    def send_z():
        for i in Z_ORDER:
            back = REL.index(-REL[i]) if REL[i] != 4 else 7
            z_copies[back] = send(at(0, 0, (0, 1)), at(0, 0, (back, back + 1)), device(x, y, z + REL[i], c))

    def send_x(k, j):
        base = count[0]
        count[0] += 2
        for to in (right, left):
            send(at(0, j, CHUNKS[k]), at(1, 2 * h + j, CHUNKS[k]), to, landed.at[base + h])
        x_copies.setdefault(k, []).append(base)

    def send_core(k, xr):
        ys = pl.ds(0, 4)
        core_copies[xr][k] = send(at(xr, ys, CHUNKS[k]), at(xr, ys, CHUNKS[k], 1), sibling)

    def after_z(k):
        chunk = CHUNKS[k]
        for i in range(*chunk):
            if i:
                z_copies[i].wait_recv()
        y_copies[k] = send(at(0, 0, chunk), at(0, 1, chunk), down), send(at(0, 0, chunk), at(0, 2, chunk), up)
        if k in FAR:
            far_copies[k] = send(at(0, 0, chunk), at(0, 3, chunk), far)
        send_x(k, 0)

    def after_y(k):
        chunk = CHUNKS[k]
        from_up, from_down = y_copies[k]
        from_up.wait_recv()
        if k % 2 and k not in FAR + TURNED:
            far_copies[k] = send(at(0, 1, chunk), at(0, 3, chunk), down)
        if k not in ACROSS:
            send_x(k, 1)
        from_down.wait_recv()
        if k % 2 == 0 and k not in FAR + TURNED:
            far_copies[k] = send(at(0, 2, chunk), at(0, 3, chunk), up)

    def turn():
        for i in Z_ORDER:
            back = REL.index(-REL[i]) if REL[i] != 4 else 7
            if any(CHUNKS[k][0] <= back < CHUNKS[k][1] for k in TURNED):
                turned[back] = send(at(0, 3, (0, 1)), at(0, 3, (back, back + 1)), device(x, y, z + REL[i], c))

    def after_far(k):
        if k in TURNED:
            for i in range(*CHUNKS[k]):
                turned[i].wait_recv()
        else:
            far_copies[k].wait_recv()
        if k == 0:
            turn()
        send_core(k, 0)

    def wait_x(k, base):
        for side in range(2):
            ref = at(1, 0, CHUNKS[k])
            pltpu.make_async_remote_copy(
                src_ref=ref, dst_ref=ref, send_sem=sent.at[0], recv_sem=landed.at[base + side],
                device_id=right, device_id_type=MESH).wait_recv()

    crossed = {}

    def cross(k):
        chunk = CHUNKS[k]
        wait_x(k, x_copies[k][0])
        crossed[k] = send(at(1, 0, chunk), at(1, 1, chunk), down), send(at(1, 0, chunk), at(1, 3, chunk), up)

    def after_x(k):
        if k in ACROSS:
            for copy in crossed[k]:
                copy.wait_recv()
        else:
            for base in x_copies[k]:
                wait_x(k, base)
        send_core(k, 1)

    send_z()
    after_z(0)
    lat_copy.wait_recv()
    activate(1 - h, 0)
    after_z(1)
    after_y(0)
    after_far(0)
    activate(1 - h, 1)
    after_z(2)
    after_y(1)
    after_z(3)
    cross(1)
    after_y(2)
    after_far(1)
    after_x(0)
    after_y(3)
    after_x(1)
    after_far(2)
    after_x(2)
    after_far(3)
    after_x(3)

    def weights(dy, base, half):
        t0 = held[c, half, :, :, base + 16 * dy : base + 16 * dy + 16].reshape(512, 128)
        t1 = held[1 - c, half, :, :, base + 16 * dy : base + 16 * dy + 16].reshape(512, 128)
        owner, row = ((c, 48), (c, 64), (1 - c, 64))[dy]
        t2 = held[owner, half, :, :, row : row + 16].reshape(512, 128)
        return jnp.concatenate([t0, t1, t2], axis=1)

    def convolve(rows, base, half):
        for dy in range(3):
            left_side = lhs[pl.ds(h + dy, rows), :, 512 * half : 512 * half + 512].reshape(128 * rows, 512)
            product = jnp.dot(left_side, weights(dy, base, half), preferred_element_type=F32)
            if dy or half:
                acc[0 : 128 * rows] += product
            else:
                acc[0 : 128 * rows] = product

    for copy in core_copies[0].values():
        copy.wait_recv()
    convolve(3, 0, 0)
    for copy in core_copies[1].values():
        copy.wait_recv()
    convolve(3, 0, 1)

    offset = vector(2) + vector(6)
    for r in range(3):
        hidden = acc[128 * r : 128 * r + 128, 0:320] + offset
        lhs[r + 1] = expand(silu_norm(hidden, m2, r2, vector(3), vector(4)).astype(BF), pick[...], tap_lane)
    lhs[4] = jnp.zeros((128, 1024), BF)
    convolve(2, 80, 0)
    convolve(2, 80, 1)
    for r in range(2):
        rows = acc[128 * r : 128 * r + 128]
        result = jnp.concatenate([rows[:, 0:256], rows[:, 320:384]], axis=1)
        out_ref[r] = ((result + vector(5) + sample[2 * h + r]).T).astype(BF)
    for copy in swaps + [lat_copy] + copies:
        copy.wait_send()


def shards(latents, mean_one, rstd_one, gain_one, shift_one, kernel_one, bias_one, embed_bias,
           mean_two, rstd_two, gain_two, shift_two, kernel_two, bias_two):
    lat = jnp.transpose(latents[0], (0, 2, 1))
    k1 = jnp.transpose(kernel_one, (1, 0, 2))
    k2 = jnp.transpose(kernel_two, (1, 0, 2))
    vmem = pl.BlockSpec(memory_space=pltpu.VMEM)
    pin = lambda v: pltpu.with_memory_space_constraint(v, pltpu.HBM)
    out = pl.pallas_call(
        kernel,
        out_shape=jax.ShapeDtypeStruct((2, 320, 128), BF),
        in_specs=[pl.BlockSpec(memory_space=pltpu.HBM)] * 14,
        out_specs=vmem,
        scratch_shapes=[
            pltpu.VMEM((2, 2, 320, 128), BF),
            pltpu.VMEM((2, 9, 4, 200), BF),
            pltpu.VMEM((8, 320), F32),
            pltpu.VMEM((4, 1, 32), F32),
            pltpu.VMEM((4, 2, 16, 256), BF),
            pltpu.VMEM((8, 2, 16, 256), BF),
            pltpu.VMEM((2, 2, 4, 8, SLOT, 128), BF),
            pltpu.VMEM((6, 128, 1024), BF),
            pltpu.VMEM((4, 128, 320), F32),
            pltpu.VMEM((320, 1024), BF),
            pltpu.VMEM((384, 384), F32),
            pltpu.SemaphoreType.DMA, pltpu.SemaphoreType.DMA,
            pltpu.SemaphoreType.DMA((7,)), pltpu.SemaphoreType.DMA((7,)),
            pltpu.SemaphoreType.DMA((COPIES,)), pltpu.SemaphoreType.DMA((COPIES,)),
            pltpu.SemaphoreType.DMA((14,)),
        ],
        compiler_params=pltpu.CompilerParams(
            collective_id=0, has_side_effects=True, vmem_limit_bytes=40 * 2**20),
        name="residual_block",
    )(*map(pin, (lat, mean_one, rstd_one, gain_one, shift_one, k1, bias_one, embed_bias,
      mean_two, rstd_two, gain_two, shift_two, k2, bias_two)))
    return jnp.transpose(out, (0, 2, 1))[None]


def solution(mesh):
    placed = (
        P("dp", "rows", None, None), P("dp", None), P("dp", None), P(), P(), P(None, None, "dp"), P(),
        P("dp", None), P("dp", None), P("dp", None), P(), P(), P(None, None, "dp"), P(),
    )
    return jax.shard_map(
        shards, mesh=mesh, in_specs=placed, out_specs=P("dp", "rows", None, None), check_vma=False
    )
```
